32 devices in a mesh: dp: 16 (over z, y, x), tensor: 2 (over core).
Axes of the slice: x: 2, y: 2, z: 4, core: 2. Of those that a mesh axis runs over, the one named last changes fastest.
Arguments:
- tokens: bfloat16 [4096, 2048], P('dp', 'tensor'), may hold values from -6 to 6
- cotangent: bfloat16 [4096, 2048], P('dp', 'tensor'), may hold values from -6 to 6
- lengths: int32 [32], replicated, may hold values from 64 to 192, as said below
- order: int32 [32], replicated, may hold values from 0 to 31, as said below
- attn_gain: bfloat16 [2048], P('tensor'), may hold values from 0.5 to 1.5
- w_query: bfloat16 [2048, 2048], P('dp', 'tensor'), may hold values from -0.125 to 0.125
- w_key: bfloat16 [2048, 1024], P('dp', 'tensor'), may hold values from -0.125 to 0.125
- w_value: bfloat16 [2048, 1024], P('dp', 'tensor'), may hold values from -0.125 to 0.125
- w_output: bfloat16 [2048, 2048], P('tensor', 'dp'), may hold values from -0.75 to 0.75
- ffn_gain: bfloat16 [2048], P('tensor'), may hold values from 0.5 to 1.5
- w_gate: bfloat16 [2048, 8192], P('dp', 'tensor'), may hold values from -0.125 to 0.125
- w_up: bfloat16 [2048, 8192], P('dp', 'tensor'), may hold values from -0.125 to 0.125
- w_down: bfloat16 [8192, 2048], P('tensor', 'dp'), may hold values from -0.0625 to 0.0625
Outputs:
- output: bfloat16 [4096, 2048], P('dp', 'tensor')
- tokens_grad: bfloat16 [4096, 2048], P('dp', 'tensor')
- attn_gain_grad: float32 [2, 1024], P('tensor', 'dp')
- query_grad: float32 [2048, 2048], P('dp', 'tensor')
- key_grad: float32 [2048, 1024], P('dp', 'tensor')
- value_grad: float32 [2048, 1024], P('dp', 'tensor')
- out_proj_grad: float32 [2048, 2048], P('tensor', 'dp')
- ffn_gain_grad: float32 [2, 1024], P('tensor', 'dp')
- gate_grad: float32 [2048, 8192], P('dp', 'tensor')
- up_grad: float32 [2048, 8192], P('dp', 'tensor')
- down_grad: float32 [8192, 2048], P('tensor', 'dp')
The draws below stay inside these ranges and needn't reach their ends.
Inputs may be any that keep to these rules, and one draw needn't show every extreme that they name: `lengths`: sequences order[2g] and order[2g+1] form data group g and have 256 tokens together; sequences lie in input order, each after the one before it. `order`: A permutation of the 32 sequence numbers.
All inputs are finite; a program needn't handle non-finite values.
Results may differ from the reference program's by a relative error of at most 0.015.
Values may be sent and summed in bfloat16 or wider, within the bound.
A program may use at most 320 MiB of HBM per device.

```python
import jax
import jax.numpy as jnp
from jax import lax

D = 2048
HEADS = 8
KV = 4
HD = 256
FF = 8192
TOK_GROUP = 256
MIN_LEN = 64
SEQS = 32
TOKENS = 4096
N_TENSOR = 2


def shared_layout(key):
    key_len, key_perm, key_top = jax.random.split(key, 3)
    groups = SEQS // 2
    first_len = jax.random.randint(key_len, (groups,), MIN_LEN, TOK_GROUP - MIN_LEN + 1, dtype=jnp.int32)
    longest = jax.random.randint(key_top, (), 0, groups, dtype=jnp.int32)
    first_len = jnp.where(jnp.arange(groups, dtype=jnp.int32) == longest, TOK_GROUP - MIN_LEN, first_len)
    work_len = jnp.stack([first_len, TOK_GROUP - first_len], axis=1).reshape(-1)
    order = jax.random.permutation(key_perm, SEQS).astype(jnp.int32)
    lengths = jnp.zeros((SEQS,), jnp.int32).at[order].set(work_len)
    return (lengths, order)


def draw_lengths(key, part):
    shared = shared_layout(key)
    return shared[0]


def draw_order(key, part):
    shared = shared_layout(key)
    return shared[1]


def block_scale(own_key, extent, shards, low, top_value):
    factor_of = 1.0
    for dim, blocks in shards:
        draws = jax.random.uniform(jax.random.fold_in(jax.random.fold_in(own_key, 6), dim), (blocks,), jnp.float32, low / len(shards), top_value / len(shards))
        factor_of = factor_of * jnp.repeat(jnp.exp(draws), extent[dim] // blocks).reshape((-1,) + (1,) * (len(extent) - 1 - dim))
    return factor_of


def normal_values(own_key, shape, width, reach, cuts=(), kind=jnp.bfloat16):
    drawn = jax.random.normal(own_key, shape, jnp.float32) * width
    if len(cuts) > 0:
        drawn = block_scale(own_key, shape, cuts, -0.22, 0.18) * drawn
    return jnp.clip(drawn, min=-reach, max=reach).astype(kind)


def setup_inputs(seed: int = 0) -> dict:
    seeds = jax.random.split(jax.random.key(seed), 14)
    return {
        "tokens": normal_values(seeds[0], (TOKENS, D), 1.0, 6.0, ((0, 16), (1, 2))),
        "cotangent": normal_values(seeds[1], (TOKENS, D), 1.0, 6.0, ((0, 16), (1, 2))),
        "lengths": draw_lengths(jax.random.fold_in(seeds[13], 71), 0),
        "order": draw_order(jax.random.fold_in(seeds[13], 71), 0),
        "attn_gain": jnp.clip(1.0 + 0.1 * jax.random.normal(seeds[4], (D,), jnp.float32), 0.5, 1.5).astype(jnp.bfloat16),
        "w_query": normal_values(seeds[5], (D, HEADS * HD), D ** -0.5, 0.125, ((0, 16), (1, 2))),
        "w_key": normal_values(seeds[6], (D, KV * HD), D ** -0.5, 0.125, ((0, 16), (1, 2))),
        "w_value": normal_values(seeds[7], (D, KV * HD), D ** -0.5, 0.125, ((0, 16), (1, 2))),
        "w_output": normal_values(seeds[8], (HEADS * HD, D), (HEADS * HD // 32) ** -0.5, 0.75, ((0, 2), (1, 16))),
        "ffn_gain": jnp.clip(1.0 + 0.1 * jax.random.normal(seeds[9], (D,), jnp.float32), 0.5, 1.5).astype(jnp.bfloat16),
        "w_gate": normal_values(seeds[10], (D, FF), D ** -0.5, 0.125, ((0, 16), (1, 2))),
        "w_up": normal_values(seeds[11], (D, FF), D ** -0.5, 0.125, ((0, 16), (1, 2))),
        "w_down": normal_values(seeds[12], (FF, D), FF ** -0.5, 0.0625, ((0, 2), (1, 16))),
    }


EPSILON = 1e-06
ROPE_BASE = 1000042.0
HIGHEST = lax.Precision.HIGHEST

@jax.custom_vjp
def low(v):
    return lax.optimization_barrier(v.astype(jnp.bfloat16)).astype(jnp.float32)

@jax.custom_vjp
def low_back(v):
    return v

def low_keep(v):
    return (low(v), None)

def low_pass(kept, grad):
    return (grad,)

def back_keep(v):
    return (v, None)

def back_low(kept, grad):
    return (low(grad),)
low.defvjp(low_keep, low_pass)
low_back.defvjp(back_keep, back_low)

def matmul(left, right):
    return jnp.dot(left, right, precision=HIGHEST)

def rotary_tables(positions):
    exponents = jnp.arange(0, HD, 2).astype(jnp.float32) / HD
    inverse = jnp.power(jnp.float32(ROPE_BASE), -exponents)
    angles = positions.astype(jnp.float32)[:, None] * inverse[None, :]
    angles = jnp.concatenate([angles, angles], axis=1)
    return (jnp.cos(angles), jnp.sin(angles))

def rotate(vectors, cosine, sine):
    middle = vectors.shape[-1] // 2
    turned = jnp.concatenate([-vectors[..., middle:], vectors[..., :middle]], axis=-1)
    return vectors * cosine + turned * sine

def work_layout(lengths, order):
    seq_ids = jnp.arange(SEQS).astype(jnp.int32)
    in_start = (jnp.cumsum(lengths) - lengths).astype(jnp.int32)
    matches = order[:, None] == seq_ids[None, :]
    work_len = lax.optimization_barrier(jnp.sum(jnp.where(matches, lengths[None, :], 0), axis=1)).astype(jnp.int32)
    work_src = lax.optimization_barrier(jnp.sum(jnp.where(matches, in_start[None, :], 0), axis=1)).astype(jnp.int32)
    pair_len = work_len.reshape(SEQS // 2, 2)
    pair_start = (jnp.cumsum(pair_len, axis=1) - pair_len).astype(jnp.int32)
    pair_src = work_src.reshape(SEQS // 2, 2)
    row_ids = jnp.arange(TOK_GROUP).astype(jnp.int32)
    slot_ids = lax.optimization_barrier(jnp.sum((row_ids[None, :, None] >= pair_start[:, None, :]).astype(jnp.int32), axis=2)) - 1
    chosen = slot_ids[:, :, None] == jnp.arange(2).astype(jnp.int32)[None, None, :]
    base_row = lax.optimization_barrier(jnp.sum(jnp.where(chosen, pair_start[:, None, :], 0), axis=2))
    positions = row_ids[None, :] - base_row
    sources = lax.optimization_barrier(jnp.sum(jnp.where(chosen, pair_src[:, None, :], 0), axis=2)) + positions
    return (sources.astype(jnp.int32), slot_ids.astype(jnp.int32), positions.astype(jnp.int32))

def group_forward(params, tokens_group, slot_ids, positions):
    attn_gain, w_query, w_key, w_value, w_output, ffn_gain, w_gate, w_up, w_down = params
    count = tokens_group.shape[0]
    row_ids = jnp.arange(count)
    rms_one = lax.rsqrt(lax.optimization_barrier(jnp.mean(tokens_group * tokens_group, axis=-1, keepdims=True)) + EPSILON)
    normed_attn = low(tokens_group * rms_one * attn_gain)
    queries = low_back(matmul(normed_attn, w_query))
    keys = low_back(matmul(normed_attn, w_key))
    values = low(low_back(matmul(normed_attn, w_value)))
    cosine, sine = rotary_tables(positions)
    queries_rot = low(rotate(queries.reshape(count, HEADS, HD), cosine[:, None, :], sine[:, None, :]))
    keys_rot = low(rotate(keys.reshape(count, KV, HD), cosine[:, None, :], sine[:, None, :]))
    grouped = queries_rot.reshape(count, KV, HEADS // KV, HD)
    scores = low_back(jnp.einsum('qgrd,kgd->grqk', grouped, keys_rot, precision=HIGHEST) * HD ** (-0.5))
    allowed = (slot_ids[:, None] == slot_ids[None, :]) & (row_ids[:, None] >= row_ids[None, :])
    masked = jnp.where(allowed[None, None], scores, -1e+30)
    highest = lax.optimization_barrier(jnp.max(masked, axis=-1, keepdims=True))
    expo = jnp.exp(masked - highest)
    probs = expo / lax.optimization_barrier(jnp.sum(expo, axis=-1, keepdims=True))
    probs_low = low(probs)
    attended = low(low_back(jnp.einsum('grqk,kgd->qgrd', probs_low, values.reshape(count, KV, HD), precision=HIGHEST)))
    attn_out = low_back(matmul(attended.reshape(count, HEADS * HD), w_output))
    mixed = tokens_group + attn_out
    rms_two = lax.rsqrt(lax.optimization_barrier(jnp.mean(mixed * mixed, axis=-1, keepdims=True)) + EPSILON)
    normed_ffn = low(mixed * rms_two * ffn_gain)
    gate = low_back(matmul(normed_ffn, w_gate))
    upward = low_back(matmul(normed_ffn, w_up))
    hidden = low(jax.nn.silu(gate) * upward)
    return mixed + matmul(hidden, w_down)

def reference(tokens, cotangent, lengths, order, attn_gain, w_query, w_key, w_value, w_output, ffn_gain, w_gate, w_up, w_down):
    params = tuple((item.astype(jnp.float32) for item in (attn_gain, w_query, w_key, w_value, w_output, ffn_gain, w_gate, w_up, w_down)))
    sources, slot_ids, positions = work_layout(lengths, order)
    tokens_work = tokens.astype(jnp.float32)[sources]
    cot_work = cotangent.astype(jnp.float32)[sources]
    zeros = jax.tree.map(jnp.zeros_like, params)

    def step(totals, inputs):
        tok_group, cot_group, slot_group, pos_group = inputs
        result, pullback = jax.vjp(lambda weights, acts: group_forward(weights, acts, slot_group, pos_group), params, tok_group)
        param_grads, acts_grad = pullback(cot_group)
        totals = jax.tree.map(lambda left, right: left + right, totals, param_grads)
        return (totals, (result, acts_grad))
    totals, (results, work_grad) = lax.scan(step, zeros, (tokens_work, cot_work, slot_ids, positions))
    flat = sources.reshape(-1)
    output = jnp.zeros((TOKENS, D), jnp.float32).at[flat].set(results.reshape(-1, D))
    tokens_grad = jnp.zeros((TOKENS, D), jnp.float32).at[flat].set(work_grad.reshape(-1, D))
    attn_gain_grad, query_grad, key_grad, value_grad, out_proj_grad, ffn_gain_grad, gate_grad, up_grad, down_grad = totals
    return (output.astype(jnp.bfloat16), tokens_grad.astype(jnp.bfloat16), attn_gain_grad.reshape(N_TENSOR, D // N_TENSOR), query_grad, key_grad, value_grad, out_proj_grad, ffn_gain_grad.reshape(N_TENSOR, D // N_TENSOR), gate_grad, up_grad, down_grad)
```

```python
import jax
import jax.numpy as jnp
from jax import lax
from jax.sharding import PartitionSpec as P

HD = 256
HALO = 192
LINE = 4

EPSILON = 1e-06
ROPE_BASE = 1000042.0
BF16 = jnp.bfloat16
F32 = jnp.float32


def matmul(left, right):
    return jnp.dot(left, right, preferred_element_type=F32)


def matmul_t(left, right):
    return lax.dot_general(left, right, (((1,), (1,)), ((), ())), preferred_element_type=F32)


def t_matmul(left, right):
    return lax.dot_general(left, right, (((0,), (0,)), ((), ())), preferred_element_type=F32)


def rotary_tables(positions):
    exponents = jnp.arange(0, HD, 2).astype(F32) / HD
    inverse = jnp.power(F32(ROPE_BASE), -exponents)
    angles = positions.astype(F32)[:, None] * inverse[None, :]
    angles = jnp.concatenate([angles, angles], axis=1)
    return (jnp.cos(angles), jnp.sin(angles))


def rotate(vectors, cosine, sine):
    middle = vectors.shape[-1] // 2
    turned = jnp.concatenate([-vectors[..., middle:], vectors[..., :middle]], axis=-1)
    return vectors * cosine + turned * sine


def rotate_back(grads, cosine, sine):
    middle = grads.shape[-1] // 2
    scaled = grads * sine
    turned = jnp.concatenate([scaled[..., middle:], -scaled[..., :middle]], axis=-1)
    return grads * cosine + turned


class Links:
    def __init__(self):
        self.count = lax.axis_size("dp")
        self.plane = self.count // LINE
        self.index = lax.axis_index("dp")
        self.line, self.place = self.index // self.plane, self.index % self.plane
        self.half = lax.axis_index("tensor")
        self.bits = [1 << b for b in range(self.plane.bit_length() - 1)]

    def step(self, x, k):
        n, shift = self.count, k * self.plane
        return lax.ppermute(x, "dp", [(d, (d + shift) % n) for d in range(n)])

    def cross(self, x, bit):
        return lax.ppermute(x, "dp", [(d, d ^ bit) for d in range(self.count)])

    def swap(self, x):
        return lax.ppermute(x, "tensor", [(0, 1), (1, 0)])

    def both(self, x):
        other = self.swap(x)
        first = self.half == 0
        return jnp.concatenate([jnp.where(first, x, other), jnp.where(first, other, x)], axis=1)

    def halves(self, x):
        width = x.shape[1] // 2
        mine = lax.dynamic_slice_in_dim(x, self.half * width, width, 1)
        theirs = lax.dynamic_slice_in_dim(x, (1 - self.half) * width, width, 1)
        return mine, theirs

    def order(self, turn):
        return self.bits[turn % len(self.bits):] + self.bits[: turn % len(self.bits)]

    def spread(self, x, turn):
        held = {0: x}
        for bit in self.order(turn):
            held |= {key | bit: self.cross(part, bit) for key, part in held.items()}
        return held

    def fold(self, held, turn):
        for bit in self.order(turn):
            kept = {key: part for key, part in held.items() if not key & bit}
            for key in kept:
                got = self.cross(held[key | bit].astype(BF16), bit)
                kept[key] = kept[key].astype(F32) + got.astype(F32)
            held = kept
        return held[0]


def gather_pieces(links, pieces, rows):
    columns = pieces[0].shape[1]
    whole = jnp.zeros((LINE, links.plane, rows, columns), BF16)
    for k, piece in enumerate(pieces):
        origin = (links.line - k) % LINE
        for key, part in links.spread(piece, k).items():
            whole = lax.dynamic_update_slice(
                whole, part[None, None], (origin, links.place ^ key, 0, 0)
            )
    return whole.reshape(-1, columns)


def fold_plane(links, grads, rows):
    columns = grads.shape[1]
    parts = grads.reshape(LINE, links.plane, rows, columns)
    out = []
    for turn in range(2):
        half = parts[turn * 2 : turn * 2 + 2]
        held = {
            key: lax.dynamic_slice_in_dim(half, links.place ^ key, 1, 1)[:, 0]
            for key in range(links.plane)
        }
        out.append(links.fold(held, turn))
    return jnp.concatenate(out, axis=0)


def on_device(
    tokens,
    cotangent,
    lengths,
    order,
    attn_gain,
    w_query,
    w_key,
    w_value,
    w_output,
    ffn_gain,
    w_gate,
    w_up,
    w_down,
):
    links = Links()
    half_index = links.half
    count, half_width = tokens.shape
    width = 2 * half_width
    rows = w_query.shape[0]
    ff_half = w_gate.shape[1]
    chunk = ff_half // LINE

    attn_mine = jnp.concatenate([w_query, w_key, w_value, w_output.T], axis=1)
    attn_all = gather_pieces(
        links, [attn_mine] + [links.step(attn_mine, k) for k in range(1, LINE)], rows
    )
    ffn_mine = jnp.stack(
        [w_gate.reshape(rows, LINE, chunk), w_up.reshape(rows, LINE, chunk), w_down.T.reshape(rows, LINE, chunk)],
        axis=2,
    ).reshape(rows, LINE, 3 * chunk)

    def for_line(k):
        target = (links.line + k) % LINE
        return lax.dynamic_slice_in_dim(ffn_mine, target, 1, 1)[:, 0]

    ffn_all = gather_pieces(
        links, [for_line(0)] + [links.step(for_line(k), k) for k in range(1, LINE)], rows
    )
    w_gate_up, w_down_t = ffn_all[:, : 2 * chunk], ffn_all[:, 2 * chunk :]

    def line_gather(x):
        return jnp.concatenate([x] + [links.step(x, k) for k in range(1, LINE)], axis=0)

    def line_sum(x):
        parts = x.reshape(LINE, count, half_width)
        total = parts[0].astype(F32)
        for k in range(1, LINE):
            total += links.step(parts[k].astype(BF16), LINE - k).astype(F32)
        return total

    n = links.count
    before = lax.ppermute(tokens[count - HALO :], "dp", [(d, d + 1) for d in range(n - 1)])
    tokens_ext = links.both(jnp.concatenate([before, tokens], axis=0)).astype(F32)
    cot_line = links.both(line_gather(cotangent))

    seq_ids = jnp.arange(lengths.shape[0])
    in_start = jnp.sum(jnp.where(seq_ids[None, :] < seq_ids[:, None], lengths[None, :], 0), axis=1)
    row_ids = links.index * count - HALO + jnp.arange(HALO + count)
    seq_of_row = jnp.sum((row_ids[:, None] >= in_start[None, :]).astype(jnp.int32), axis=1) - 1
    chosen = seq_of_row[:, None] == seq_ids[None, :]
    positions = row_ids - jnp.sum(jnp.where(chosen, in_start[None, :], 0), axis=1)
    cosine, sine = rotary_tables(positions)
    cos_k, sin_k = cosine[:, None, :], sine[:, None, :]
    cos_q, sin_q = cosine[HALO:, None, None, :], sine[HALO:, None, None, :]

    gain_one = links.both(attn_gain[None, :]).astype(F32)
    gain_two = ffn_gain.astype(F32)[None, :]
    rms_one = lax.rsqrt(jnp.mean(tokens_ext * tokens_ext, axis=-1, keepdims=True) + EPSILON)
    normed_attn = (tokens_ext * rms_one * gain_one).astype(BF16)

    q_width, k_width = w_query.shape[1], w_key.shape[1]
    kv_local = k_width // HD
    repeats = q_width // k_width
    ext = HALO + count
    w_q = attn_all[:, :q_width]
    w_kv = attn_all[:, q_width : q_width + 2 * k_width]
    w_out_t = attn_all[:, q_width + 2 * k_width :]
    queries = matmul(normed_attn[HALO:], w_q).reshape(count, kv_local, repeats, HD)
    keys_values = matmul(normed_attn, w_kv)
    keys = keys_values[:, :k_width].reshape(ext, kv_local, HD)
    values = keys_values[:, k_width:].astype(BF16).reshape(ext, kv_local, HD)
    queries_rot = rotate(queries, cos_q, sin_q).astype(BF16)
    keys_rot = rotate(keys, cos_k, sin_k).astype(BF16)
    allowed = (seq_of_row[HALO:, None] == seq_of_row[None, :]) & (
        row_ids[HALO:, None] >= row_ids[None, :]
    )
    scores = jnp.einsum("qgrd,kgd->grqk", queries_rot, keys_rot, preferred_element_type=F32)
    scores = jnp.where(allowed[None, None], scores * HD ** (-0.5), -1e30)
    highest = jnp.max(scores, axis=-1, keepdims=True)
    expo = jnp.exp(scores - highest)
    probs = expo / jnp.sum(expo, axis=-1, keepdims=True)
    probs_low = probs.astype(BF16)
    attended = jnp.einsum("grqk,kgd->qgrd", probs_low, values, preferred_element_type=F32)
    attended = attended.astype(BF16).reshape(count, q_width)
    out_mine, out_theirs = links.halves(matmul_t(attended, w_out_t))
    tokens_half = tokens.astype(F32)
    mixed = tokens_half + (out_mine + links.swap(out_theirs))

    def row_sum(x):
        total = jnp.sum(x, axis=-1)[None, :]
        return (total + links.swap(total)).reshape(count, 1)

    rms_two = lax.rsqrt(row_sum(mixed * mixed) / width + EPSILON)
    normed_ffn = links.both(line_gather((mixed * rms_two * gain_two).astype(BF16)))

    gate_up = matmul(normed_ffn, w_gate_up)
    gate, upward = gate_up[:, :chunk], gate_up[:, chunk:]
    sigmoid = jax.nn.sigmoid(gate)
    silu_gate = gate * sigmoid
    hidden = (silu_gate * upward).astype(BF16)
    hidden_grad = matmul(cot_line, w_down_t)
    gate_act_grad = (hidden_grad * upward * sigmoid * (1.0 + gate * (1.0 - sigmoid))).astype(BF16)
    up_act_grad = (hidden_grad * silu_gate).astype(BF16)
    act_grad = jnp.concatenate([gate_act_grad, up_act_grad], axis=1)
    norm_mine, norm_theirs = links.halves(matmul_t(act_grad, w_gate_up))
    normed_ffn_grad = line_sum(norm_mine + links.swap(norm_theirs.astype(BF16)).astype(F32))
    ffn_mine_out, ffn_theirs_out = links.halves(matmul_t(hidden, w_down_t))
    ffn_out = line_sum(ffn_mine_out + links.swap(ffn_theirs_out.astype(BF16)).astype(F32))
    output = (mixed + ffn_out).astype(BF16)

    down_sum = fold_plane(links, t_matmul(cot_line, hidden).astype(BF16), rows)
    gate_up_sum = fold_plane(links, t_matmul(normed_ffn, act_grad).astype(BF16), rows)
    ffn_sum = jnp.concatenate([gate_up_sum, down_sum], axis=2).astype(BF16)
    ffn_grads = jnp.zeros((3, rows, LINE, chunk), F32)
    for k in range(LINE):
        part = lax.dynamic_slice_in_dim(ffn_sum, (links.line + k) % LINE, 1, 0)[0]
        if k:
            part = links.step(part, k)
        part = part.astype(F32).reshape(rows, 3, chunk).transpose(1, 0, 2)
        ffn_grads = lax.dynamic_update_slice(
            ffn_grads, part[:, :, None], (0, 0, (links.line - k) % LINE, 0)
        )
    ffn_grads = ffn_grads.reshape(3, rows, ff_half)

    ffn_gain_local = jnp.sum(normed_ffn_grad * mixed * rms_two, axis=0)
    inner_two = row_sum(normed_ffn_grad * gain_two * mixed)
    mixed_grad = (
        cotangent.astype(F32)
        + rms_two * gain_two * normed_ffn_grad
        - mixed * rms_two * rms_two * rms_two * inner_two / width
    )

    attn_out_grad = links.both(mixed_grad.astype(BF16))
    out_local = t_matmul(attn_out_grad, attended)
    attended_grad = matmul(attn_out_grad, w_out_t).astype(BF16)
    attended_grad = attended_grad.reshape(count, kv_local, repeats, HD)
    values_grad = jnp.einsum("grqk,qgrd->kgd", probs_low, attended_grad, preferred_element_type=F32)
    values_grad = values_grad.astype(BF16).reshape(ext, k_width)
    probs_grad = jnp.einsum("qgrd,kgd->grqk", attended_grad, values, preferred_element_type=F32)
    scores_grad = (
        probs * (probs_grad - jnp.sum(probs * probs_grad, axis=-1, keepdims=True))
    ).astype(BF16)
    rot_q_grad = jnp.einsum(
        "grqk,kgd->qgrd", scores_grad, keys_rot, preferred_element_type=F32
    ) * HD ** (-0.5)
    rot_k_grad = jnp.einsum(
        "grqk,qgrd->kgd", scores_grad, queries_rot, preferred_element_type=F32
    ) * HD ** (-0.5)
    queries_grad = rotate_back(rot_q_grad, cos_q, sin_q).astype(BF16).reshape(count, q_width)
    keys_grad = rotate_back(rot_k_grad, cos_k, sin_k).astype(BF16).reshape(ext, k_width)
    kv_grad = jnp.concatenate([keys_grad, values_grad], axis=1)
    attn_local = jnp.concatenate(
        [t_matmul(normed_attn[HALO:], queries_grad), t_matmul(normed_attn, kv_grad), out_local],
        axis=1,
    )
    attn_sum = fold_plane(links, attn_local.astype(BF16), rows)
    attn_total = lax.dynamic_slice_in_dim(attn_sum, links.line, 1, 0)[0]
    for k in range(1, LINE):
        part = lax.dynamic_slice_in_dim(attn_sum, (links.line + k) % LINE, 1, 0)[0]
        attn_total += links.step(part.astype(BF16), k).astype(F32)

    normed_grad = matmul_t(kv_grad, w_kv)
    normed_grad = normed_grad + jnp.pad(matmul_t(queries_grad, w_q), ((HALO, 0), (0, 0)))
    grad_mine, grad_theirs = links.halves(normed_grad)
    grad_half = grad_mine + links.swap(grad_theirs.astype(BF16)).astype(F32)
    behind = lax.ppermute(grad_half[:HALO].astype(BF16), "dp", [(d + 1, d) for d in range(n - 1)])
    normed_attn_grad = grad_half[HALO:] + jnp.pad(behind.astype(F32), ((count - HALO, 0), (0, 0)))
    rms_mine = rms_one[HALO:]
    gain_mine = attn_gain.astype(F32)[None, :]
    attn_gain_local = jnp.sum(normed_attn_grad * tokens_half * rms_mine, axis=0)
    inner_one = row_sum(normed_attn_grad * gain_mine * tokens_half)
    tokens_grad = (
        mixed_grad
        + rms_mine * gain_mine * normed_attn_grad
        - tokens_half * rms_mine * rms_mine * rms_mine * inner_one / width
    ).astype(BF16)

    gains = jnp.stack([attn_gain_local, ffn_gain_local])
    gains = lax.psum_scatter(gains, "dp", scatter_dimension=1, tiled=True)
    return (
        output,
        tokens_grad,
        gains[:1],
        attn_total[:, :q_width],
        attn_total[:, q_width : q_width + k_width],
        attn_total[:, q_width + k_width : q_width + 2 * k_width],
        attn_total[:, q_width + 2 * k_width :].T,
        gains[1:],
        ffn_grads[0],
        ffn_grads[1],
        ffn_grads[2].T,
    )


def solution(mesh):
    weight = P("dp", "tensor")
    turned = P("tensor", "dp")
    return jax.shard_map(
        on_device,
        mesh=mesh,
        in_specs=(
            weight, weight, P(), P(), P("tensor"), weight, weight, weight, turned,
            P("tensor"), weight, weight, turned,
        ),
        out_specs=(
            weight, weight, turned, weight, weight, weight, turned, turned, weight, weight, turned,
        ),
        check_vma=False,
    )
```

```python
import functools

import jax
import jax.experimental.pallas as pl
import jax.experimental.pallas.tpu as pltpu
import jax.numpy as jnp
from jax import lax
from jax.sharding import PartitionSpec as P

HD = 256
HALO = 192
LINE = 4

EPSILON = 1e-06
ROPE_BASE = 1000042.0
BF16 = jnp.bfloat16
F32 = jnp.float32
MESH = pl.DeviceIdType.MESH
ANY = pl.BlockSpec(memory_space=pl.ANY)


def matmul(left, right):
    return jnp.dot(left, right, preferred_element_type=F32)


def matmul_t(left, right):
    return lax.dot_general(left, right, (((1,), (1,)), ((), ())), preferred_element_type=F32)


def t_matmul(left, right):
    return lax.dot_general(left, right, (((0,), (0,)), ((), ())), preferred_element_type=F32)


def rotary_tables(positions):
    exponents = jnp.arange(0, HD, 2).astype(F32) / HD
    inverse = jnp.power(F32(ROPE_BASE), -exponents)
    angles = positions.astype(F32)[:, None] * inverse[None, :]
    angles = jnp.concatenate([angles, angles], axis=1)
    return (jnp.cos(angles), jnp.sin(angles))


def rotate(vectors, cosine, sine):
    middle = vectors.shape[-1] // 2
    turned = jnp.concatenate([-vectors[..., middle:], vectors[..., :middle]], axis=-1)
    return vectors * cosine + turned * sine


def rotate_back(grads, cosine, sine):
    middle = grads.shape[-1] // 2
    scaled = grads * sine
    turned = jnp.concatenate([scaled[..., middle:], -scaled[..., :middle]], axis=-1)
    return grads * cosine + turned


class Links:
    def __init__(self):
        self.count = lax.axis_size("dp")
        self.plane = self.count // LINE
        self.index = lax.axis_index("dp")
        self.line, self.place = self.index // self.plane, self.index % self.plane
        self.half = lax.axis_index("tensor")
        self.bits = [1 << b for b in range(self.plane.bit_length() - 1)]

    def step(self, x, k):
        n, shift = self.count, k * self.plane
        return lax.ppermute(x, "dp", [(d, (d + shift) % n) for d in range(n)])

    def cross(self, x, bit):
        return lax.ppermute(x, "dp", [(d, d ^ bit) for d in range(self.count)])

    def swap(self, x):
        return lax.ppermute(x, "tensor", [(0, 1), (1, 0)])

    def both(self, x):
        other = self.swap(x)
        first = self.half == 0
        return jnp.concatenate([jnp.where(first, x, other), jnp.where(first, other, x)], axis=1)

    def halves(self, x):
        width = x.shape[1] // 2
        mine = lax.dynamic_slice_in_dim(x, self.half * width, width, 1)
        theirs = lax.dynamic_slice_in_dim(x, (1 - self.half) * width, width, 1)
        return mine, theirs

    def order(self, turn):
        return self.bits[turn % len(self.bits):] + self.bits[: turn % len(self.bits)]

    def spread(self, x, turn):
        held = {0: x}
        for bit in self.order(turn):
            held |= {key | bit: self.cross(part, bit) for key, part in held.items()}
        return held

    def fold(self, held, turn):
        for bit in self.order(turn):
            kept = {key: part for key, part in held.items() if not key & bit}
            for key in kept:
                got = self.cross(held[key | bit].astype(BF16), bit)
                kept[key] = kept[key].astype(F32) + got.astype(F32)
            held = kept
        return held[0]


def flip(place, key):
    bit = 1
    while bit <= key:
        if key & bit:
            place = place + bit * (1 - 2 * lax.rem(lax.div(place, bit), 2))
        bit *= 2
    return place


def gather_kernel(plane, wq, wk, wv, wo, wg, wu, wd, tok, attn, ffn, ext,
                  own_sem, zs, zr, ps, pr, fs, fr, ts, tr):
    rows, tok_rows, width = wq.shape[0], tok.shape[0], tok.shape[1]
    count = plane * LINE
    halo = ext.shape[0] - tok_rows
    chunk = wd.shape[1] // LINE
    bits = [1 << b for b in range(plane.bit_length() - 1)]
    device, half = lax.axis_index("dp"), lax.axis_index("tensor")
    line, place = lax.div(device, plane), lax.rem(device, plane)

    greet = [lax.rem(line + k, LINE) * plane + place for k in range(1, LINE)]
    greet += [line * plane + flip(place, bit) for bit in bits]
    greet += [lax.rem(device + 1, count), lax.rem(device + count - 1, count)]
    barrier = pltpu.get_barrier_semaphore()
    for peer in greet:
        pl.semaphore_signal(barrier, 1, device_id=(peer, half), device_id_type=MESH)
    pl.semaphore_signal(barrier, 1, device_id=(device, 1 - half), device_id_type=MESH)

    def remote(src, dst, sent, got, peer, core=half):
        return pltpu.make_async_remote_copy(
            src_ref=src, dst_ref=dst, send_sem=sent, recv_sem=got,
            device_id=(peer, core), device_id_type=MESH,
        )

    mine = pl.ds(pl.multiple_of(device * rows, rows), rows)
    own, at = [], 0
    for block in (wq, wk, wv, wo):
        wide = block.shape[1]
        own.append(pltpu.make_async_copy(block, attn.at[mine, pl.ds(at, wide)], own_sem.at[len(own)]))
        at += wide
    from_line = pl.ds(pl.multiple_of(line * rows, rows), rows)

    def hidden(block, member):
        return block.at[:, pl.ds(pl.multiple_of(member * chunk, chunk), chunk)]

    for j, block in enumerate((wg, wu, wd)):
        own.append(
            pltpu.make_async_copy(
                hidden(block, line), ffn.at[from_line, pl.ds(j * chunk, chunk)], own_sem.at[len(own)]
            )
        )
    features = pl.ds(pl.multiple_of(half * width, width), width)
    own.append(pltpu.make_async_copy(tok, ext.at[pl.ds(halo, tok_rows), features], own_sem.at[len(own)]))
    for copy in own:
        copy.start()
    first = pltpu.make_async_copy(
        tok.at[pl.ds(0, halo)], ext.at[pl.ds(0, halo), features], own_sem.at[len(own)]
    )
    pl.semaphore_wait(barrier, len(greet) + 1)

    tok_cross = remote(tok, ext.at[pl.ds(halo, tok_rows), features], ts.at[0], tr.at[0], device, 1 - half)
    tok_next = remote(
        tok.at[pl.ds(tok_rows - halo, halo)], ext.at[pl.ds(0, halo), features], ts.at[1], tr.at[1], device + 1
    )
    tok_relay = remote(
        ext.at[pl.ds(0, halo), features], ext.at[pl.ds(0, halo), features], ts.at[2], tr.at[2], device, 1 - half
    )
    for copy in own[:4]:
        copy.wait()

    def line_copy(origin, step):
        block = attn.at[pl.ds(pl.multiple_of((origin * plane + place) * rows, rows), rows)]
        return remote(block, block, zs.at[(step + 1) // 2, origin], zr.at[origin], device + step * plane)

    part = rows // 2

    def keys_after(turn, stage):
        keys = [0]
        for bit in (bits[turn:] + bits[:turn])[:stage]:
            keys += [key | bit for key in keys]
        return keys

    def plane_copy(origin, turn, key, bit):
        block = attn.at[
            pl.ds(pl.multiple_of((origin * plane + flip(place, key)) * rows + turn * part, part), part)
        ]
        sems = [s.at[origin, turn, key | bit] for s in (ps, pr)]
        return remote(block, block, *sems, line * plane + flip(place, bit))

    def spread(origin, stage):
        for turn in range(2):
            order = bits[turn:] + bits[:turn]
            if stage:
                for key in keys_after(turn, stage - 1):
                    plane_copy(origin, turn, key, order[stage - 1]).wait_recv()
            if stage < len(bits):
                for key in keys_after(turn, stage):
                    plane_copy(origin, turn, key, order[stage]).start()

    def ffn_copies(k):
        member = lax.rem(line + k, LINE)
        return [
            remote(
                hidden(block, member), ffn.at[from_line, pl.ds(j * chunk, chunk)],
                fs.at[k - 1, j], fr.at[k - 1, j], member * plane + place,
            )
            for j, block in enumerate((wg, wu, wd))
        ]

    slots = [(line, None, None)]
    for d in range(1, LINE):
        slots += [(line - d, line >= d, 1), (line + d, line + d < LINE, -1)]

    def guarded(condition, action):
        if condition is None:
            action()
        else:
            pl.when(condition)(action)

    def arrive(origin, step):
        if step is not None:
            line_copy(origin, step).wait_recv()
        if step in (None, 1):
            pl.when(line < LINE - 1)(lambda: line_copy(origin, 1).start())
        if step in (None, -1):
            pl.when(line > 0)(lambda: line_copy(origin, -1).start())
        spread(origin, 0)

    pl.when(device < count - 1)(lambda: tok_next.start())
    for j in range(len(slots) + len(bits)):
        if j < len(slots):
            origin, condition, step = slots[j]
            guarded(condition, functools.partial(arrive, origin, step))
        if j == 0:
            tok_cross.start()
        if j in (2, 4, 6):
            for copy in ffn_copies((1, 3, 2)[j // 2 - 1]):
                copy.start()
        for stage in range(1, len(bits) + 1):
            if 0 <= j - stage < len(slots):
                origin, condition, step = slots[j - stage]
                guarded(condition, functools.partial(spread, origin, stage))
        if j == 1:
            pl.when(device == 0)(lambda: first.start())
            pl.when(device == 0)(lambda: first.wait())
            pl.when(device > 0)(lambda: tok_next.wait_recv())
            tok_relay.start()

    for origin in range(LINE):
        pl.when((origin <= line) & (line < LINE - 1))(lambda o=origin: line_copy(o, 1).wait_send())
        pl.when((origin >= line) & (line > 0))(lambda o=origin: line_copy(o, -1).wait_send())
        for turn in range(2):
            order = bits[turn:] + bits[:turn]
            for stage, bit in enumerate(order):
                for key in keys_after(turn, stage):
                    plane_copy(origin, turn, key, bit).wait_send()
    for k in range(1, LINE):
        for copy in ffn_copies(k):
            copy.wait()
    pl.when(device < count - 1)(lambda: tok_next.wait_send())
    tok_cross.wait()
    tok_relay.wait()
    for copy in own[4:]:
        copy.wait()


def gather_start(plane, tokens, wq, wk, wv, wo, wg, wu, wd):
    rows = wq.shape[0]
    chunk = wd.shape[1] // LINE
    columns = sum(w.shape[1] for w in (wq, wk, wv, wo))
    dma = pltpu.SemaphoreType.DMA
    return pl.pallas_call(
        functools.partial(gather_kernel, plane),
        out_shape=(
            jax.ShapeDtypeStruct((LINE * plane * rows, columns), BF16),
            jax.ShapeDtypeStruct((LINE * rows, 3 * chunk), BF16),
            jax.ShapeDtypeStruct((HALO + tokens.shape[0], 2 * tokens.shape[1]), BF16),
        ),
        in_specs=[ANY] * 8,
        out_specs=[ANY] * 3,
        scratch_shapes=[
            dma((9,)), dma((2, LINE)), dma((LINE,)), dma((LINE, 2, plane)), dma((LINE, 2, plane)),
            dma((LINE - 1, 3)), dma((LINE - 1, 3)), dma((3,)), dma((3,)),
        ],
        compiler_params=pltpu.CompilerParams(collective_id=1, has_side_effects=True),
    )(wq, wk, wv, wo, wg, wu, wd, tokens)


def spread_plane(links, own, rows):
    columns = own.shape[1]
    own = own.reshape(LINE, rows, columns)
    whole = jnp.zeros((LINE, links.plane, rows, columns), BF16)
    for turn in range(2):
        for key, part in links.spread(own[2 * turn : 2 * turn + 2], turn).items():
            whole = lax.dynamic_update_slice(
                whole, part[:, None], (2 * turn, flip(links.place, key), 0, 0)
            )
    return whole.reshape(-1, columns)


def fold_plan(bits, turn):
    order, plan, slot = bits[turn:] + bits[:turn], [], 0
    for stage, bit in enumerate(order):
        keys = [0]
        for later in order[stage + 1 :]:
            keys += [key | later for key in keys]
        plan.append((bit, keys, slot))
        slot += len(keys)
    return plan


def finish_kernel(plane, gq, gkv, go, fsum, grad_mine, grad_theirs, mixed_grad, tok, rms, gain, gain_two,
                  total, fout, tok_grad, gains,
                  recv, sendbuf, acc, zsend, zrecv, gx, hsend, hrecv, nag, inner, inner_in, gbuf, gin,
                  own_sem, s0, r0, zs, zr, fs, fr, cs, cr, gs, gr):
    rows = total.shape[0]
    segment = gq.shape[1]
    count = plane * LINE
    tok_rows, width = tok.shape
    halo = grad_mine.shape[0] - tok_rows
    chunk = fsum.shape[2] // 3
    part = rows // 2
    bits = [1 << b for b in range(plane.bit_length() - 1)]
    device, half = lax.axis_index("dp"), lax.axis_index("tensor")
    line, place = lax.div(device, plane), lax.rem(device, plane)

    greet = [lax.rem(line + k, LINE) * plane + place for k in range(1, LINE)]
    greet += [line * plane + flip(place, bit) for bit in bits]
    greet += [lax.rem(device + 1, count), lax.rem(device + count - 1, count)]
    barrier = pltpu.get_barrier_semaphore()
    for peer in greet:
        pl.semaphore_signal(barrier, 1, device_id=(peer, half), device_id_type=MESH)
    pl.semaphore_signal(barrier, 1, device_id=(device, 1 - half), device_id_type=MESH)

    def remote(src, dst, sent, got, peer, core=half):
        return pltpu.make_async_remote_copy(
            src_ref=src, dst_ref=dst, send_sem=sent, recv_sem=got,
            device_id=(peer, core), device_id_type=MESH,
        )

    def member(c):
        return lax.rem(line + c, LINE)

    def hidden(origin):
        return pl.ds(pl.multiple_of(origin * chunk, chunk), chunk)

    def ffn_copy(c, j):
        return remote(
            fsum.at[member(c), :, pl.ds(j * chunk, chunk)], fout.at[j, :, hidden(line)],
            fs.at[c - 1, j], fr.at[c - 1, j], member(c) * plane + place,
        )

    own = [
        pltpu.make_async_copy(fsum.at[line, :, pl.ds(j * chunk, chunk)], fout.at[j, :, hidden(line)], own_sem.at[j])
        for j in range(3)
    ]
    for copy in own:
        copy.start()
    pl.semaphore_wait(barrier, len(greet) + 1)

    plans = [fold_plan(bits, turn) for turn in range(2)]
    stages, later = len(bits), plane // 2

    def raw(ref, c, turn, key):
        at = (member(c) * plane + flip(place, key)) * rows + turn * part
        return ref.at[pl.ds(pl.multiple_of(at, part), part)]

    def fold_copies(c, turn, stage):
        bit, keys, slot = plans[turn][stage]
        peer = line * plane + flip(place, bit)
        out = []
        for j, key in enumerate(keys):
            sems = (s0.at[c, turn, slot + j], r0.at[c, turn, slot + j])
            dst = recv.at[c, turn, slot + j]
            if stage == 0:
                for g, ref in enumerate((gq, gkv, go)):
                    out.append(remote(raw(ref, c, turn, key | bit), dst.at[:, pl.ds(g * segment, segment)], *sems, peer))
            else:
                out.append(remote(sendbuf.at[c, turn, slot - later + j], dst, *sems, peer))
        return out

    def fold_wait(c, turn, stage, sent):
        bit, keys, slot = plans[turn][stage]
        for j in range(len(keys)):
            whole = recv.at[c, turn, slot + j]
            copy = remote(whole, whole, s0.at[c, turn, slot + j], r0.at[c, turn, slot + j], line * plane + flip(place, bit))
            if sent:
                copy.wait_send()
            else:
                copy.wait_recv()

    step = 16

    def fold_add(c, turn, stage):
        bit, keys, slot = plans[turn][stage]
        last = stage == len(plans[turn]) - 1
        sends = {}
        if not last:
            next_bit, next_keys, next_slot = plans[turn][stage + 1]
            sends = {key | next_bit: next_slot - later + j for j, key in enumerate(next_keys)}

        def body(i, carry):
            at = pl.ds(pl.multiple_of(i * step, step), step)
            for j, key in enumerate(keys):
                for g, ref in enumerate((gq, gkv, go)):
                    columns = pl.ds(g * segment, segment)
                    got = recv[c, turn, slot + j, at, columns].astype(F32)
                    if stage == 0:
                        had = raw(ref, c, turn, key)[at, :].astype(F32)
                    else:
                        had = acc[c, turn, key_slot[key], at, columns]
                    value = had + got
                    if last and c:
                        zsend[c - 1, pl.ds(pl.multiple_of(turn * part + i * step, step), step), columns] = value.astype(BF16)
                    elif last:
                        total[pl.ds(pl.multiple_of(turn * part + i * step, step), step), columns] = value
                    elif key in sends:
                        sendbuf[c, turn, sends[key], at, columns] = value.astype(BF16)
                    else:
                        acc[c, turn, key_slot[key], at, columns] = value
            return carry

        stay = [key for key in plans[turn][0][1] if not key & plans[turn][min(1, stages - 1)][0]]
        key_slot = {key: j for j, key in enumerate(stay)}
        lax.fori_loop(0, part // step, body, 0)

    def z_copy(c, turn):
        at = pl.ds(turn * part, part)
        return remote(
            zsend.at[c - 1, at], zrecv.at[c - 1, at], zs.at[c - 1, turn], zr.at[c - 1, turn], member(c) * plane + place
        )

    core_copy = remote(grad_theirs, gx, cs.at[0], cr.at[0], device, 1 - half)
    halo_copy = remote(hsend, hrecv, cs.at[1], cr.at[1], device - 1)
    inner_copy = remote(inner, inner_in, cs.at[2], cr.at[2], device, 1 - half)
    core_copy.start()

    turns = (2, 1, 3, 0)

    def start(c, stage):
        for turn in range(2):
            for copy in fold_copies(c, turn, stage):
                copy.start()

    start(turns[0], 0)
    start(turns[1], 0)
    for c in range(1, LINE):
        for j in range(3):
            ffn_copy(c, j).start()

    core_copy.wait()

    def rows_of(i):
        return pl.ds(pl.multiple_of(i * step, step), step)

    def add_halo(i, carry):
        hsend[rows_of(i)] = (grad_mine[rows_of(i)] + gx[rows_of(i)].astype(F32)).astype(BF16)
        return carry

    def add_own(i, carry):
        at = pl.ds(pl.multiple_of(halo + i * step, step), step)
        nag[rows_of(i)] = grad_mine[at] + gx[at].astype(F32)
        return carry

    def add_behind(i, carry):
        at = pl.ds(pl.multiple_of(tok_rows - halo + i * step, step), step)
        nag[at] = nag[at] + hrecv[rows_of(i)].astype(F32)
        return carry

    def local_sums(i, carry):
        at = rows_of(i)
        grad, x = nag[at], tok[at].astype(F32)
        weighted = jnp.sum(grad * gain[...] * x, axis=1, keepdims=True)
        inner[at] = jnp.broadcast_to(weighted, (step, inner.shape[1]))
        product = grad * x * rms[at]
        return carry + product[:8] + product[8:]

    def last_norm(i, carry):
        at = rows_of(i)
        r = rms[at]
        whole = (inner[at] + inner_in[at])[:, :1]
        value = mixed_grad[at] + r * gain[...] * nag[at] - tok[at].astype(F32) * (r * r * r * whole / (2 * width))
        tok_grad[at] = value.astype(BF16)
        return carry

    def norm_first():
        lax.fori_loop(0, halo // step, add_halo, 0)
        pl.when(device > 0)(lambda: halo_copy.start())
        lax.fori_loop(0, tok_rows // step, add_own, 0)

    def norm_second():
        @pl.when(device < count - 1)
        def _():
            halo_copy.wait_recv()
            lax.fori_loop(0, halo // step, add_behind, 0)

        sums = lax.fori_loop(0, tok_rows // step, local_sums, jnp.zeros((8, width), F32))
        gbuf[...] = jnp.concatenate(
            [jnp.sum(sums, axis=0, keepdims=True), gain_two[...], jnp.zeros((6, width), F32)], axis=0
        )
        inner_copy.start()

    def gain_copy(j):
        peer = line * plane + flip(place, bits[j]) if j < stages else member(j - stages + 1) * plane + place
        return remote(gbuf, gin.at[j], gs.at[j], gr.at[j], peer)

    def norm_third():
        inner_copy.wait()
        lax.fori_loop(0, tok_rows // step, last_norm, 0)

    norm_first()

    pending = []
    for j in range(len(turns) + stages):
        if j < len(turns):
            if j + 2 < len(turns):
                start(turns[j + 2], 0)
        for stage in range(stages):
            if 0 <= j - stage < len(turns):
                c = turns[j - stage]
                for turn in range(2):
                    fold_wait(c, turn, stage, False)
                    fold_add(c, turn, stage)
                    if stage + 1 < stages:
                        for copy in fold_copies(c, turn, stage + 1):
                            copy.start()
                    elif c:
                        z_copy(c, turn).start()
        if j == 0:
            norm_second()
        elif j <= stages:
            if j > 1:
                gain_copy(j - 2).wait()
                gbuf[...] = gbuf[...] + gin[j - 2]
            gain_copy(j - 1).start()
            if j == 1:
                norm_third()

    gain_copy(stages - 1).wait()
    gbuf[...] = gbuf[...] + gin[stages - 1]
    for k in range(stages, stages + LINE - 1):
        gain_copy(k).start()
    for k in range(stages, stages + LINE - 1):
        gain_copy(k).wait()
    gains[...] = gbuf[...] + sum(gin[k] for k in range(stages, stages + LINE - 1))

    for c in range(1, LINE):
        for turn in range(2):
            z_copy(c, turn).wait()

    def add_line(i, carry):
        at = rows_of(i)
        total[at] = total[at] + sum(zrecv[c, at].astype(F32) for c in range(LINE - 1))
        return carry

    lax.fori_loop(0, rows // step, add_line, 0)
    for c in range(LINE):
        for turn in range(2):
            for stage in range(stages):
                fold_wait(c, turn, stage, True)
    for c in range(1, LINE):
        for j in range(3):
            ffn_copy(c, j).wait()
    pl.when(device > 0)(lambda: halo_copy.wait_send())
    for copy in own:
        copy.wait()


def finish(plane, gq, gkv, go, fsum, grad_mine, grad_theirs, mixed_grad, tok, rms, gain, gain_two):
    columns = 3 * gq.shape[1]
    rows, chunk = fsum.shape[1], fsum.shape[2] // 3
    part = rows // 2
    tok_rows, width = tok.shape
    bits = plane.bit_length() - 1
    dma, vmem = pltpu.SemaphoreType.DMA, pltpu.VMEM
    kept = plane - 1
    inside = pl.BlockSpec(memory_space=pltpu.VMEM)
    return pl.pallas_call(
        functools.partial(finish_kernel, plane),
        out_shape=(
            jax.ShapeDtypeStruct((rows, columns), F32),
            jax.ShapeDtypeStruct((3, rows, LINE * chunk), BF16),
            jax.ShapeDtypeStruct((tok_rows, width), BF16),
            jax.ShapeDtypeStruct((8, width), F32),
        ),
        in_specs=[inside] * 3 + [ANY] + [inside] * 7,
        out_specs=[inside, ANY, inside, inside],
        scratch_shapes=[
            vmem((LINE, 2, kept, part, columns), BF16), vmem((LINE, 2, kept - plane // 2, part, columns), BF16),
            vmem((LINE, 2, plane // 4, part, columns), F32), vmem((LINE - 1, rows, columns), BF16),
            vmem((LINE - 1, rows, columns), BF16), vmem(grad_theirs.shape, BF16), vmem((HALO, width), BF16),
            vmem((HALO, width), BF16), vmem((tok_rows, width), F32), vmem((tok_rows, 128), F32),
            vmem((tok_rows, 128), F32), vmem((8, width), F32), vmem((bits + LINE - 1, 8, width), F32),
            dma((3,)), dma((LINE, 2, kept)), dma((LINE, 2, kept)), dma((LINE - 1, 2)), dma((LINE - 1, 2)),
            dma((LINE - 1, 3)), dma((LINE - 1, 3)), dma((3,)), dma((3,)),
            dma((bits + LINE - 1,)), dma((bits + LINE - 1,)),
        ],
        compiler_params=pltpu.CompilerParams(
            collective_id=2, has_side_effects=True, vmem_limit_bytes=60 * 2**20
        ),
    )(gq, gkv, go, fsum, grad_mine, grad_theirs, mixed_grad, tok, rms, gain, gain_two)


def fold_plane(links, grads, rows):
    columns = grads.shape[1]
    parts = grads.reshape(LINE, links.plane, rows, columns)
    out = []
    for turn in range(2):
        half = parts[turn * 2 : turn * 2 + 2]
        held = {
            key: lax.dynamic_slice_in_dim(half, flip(links.place, key), 1, 1)[:, 0]
            for key in range(links.plane)
        }
        out.append(links.fold(held, turn))
    return jnp.concatenate(out, axis=0)


def on_device(
    tokens,
    cotangent,
    lengths,
    order,
    attn_gain,
    w_query,
    w_key,
    w_value,
    w_output,
    ffn_gain,
    w_gate,
    w_up,
    w_down,
):
    links = Links()
    half_index = links.half
    count, half_width = tokens.shape
    width = 2 * half_width
    rows = w_query.shape[0]
    ff_half = w_gate.shape[1]
    chunk = ff_half // LINE

    attn_all, ffn_own, tokens_ext = gather_start(
        links.plane, tokens, w_query, w_key, w_value, w_output.T, w_gate, w_up, w_down.T
    )
    ffn_all = spread_plane(links, ffn_own, rows)
    w_gate_up, w_down_t = ffn_all[:, : 2 * chunk], ffn_all[:, 2 * chunk :]

    def line_gather(x):
        return jnp.concatenate([x] + [links.step(x, k) for k in range(1, LINE)], axis=0)

    def line_sum(x):
        parts = x.reshape(LINE, count, half_width)
        total = parts[0].astype(F32)
        for k in range(1, LINE):
            total += links.step(parts[k].astype(BF16), LINE - k).astype(F32)
        return total

    n = links.count
    tokens_ext = tokens_ext.astype(F32)
    cot_line = links.both(line_gather(cotangent))

    seq_ids = jnp.arange(lengths.shape[0])
    in_start = jnp.sum(jnp.where(seq_ids[None, :] < seq_ids[:, None], lengths[None, :], 0), axis=1)
    row_ids = links.index * count - HALO + jnp.arange(HALO + count)
    seq_of_row = jnp.sum((row_ids[:, None] >= in_start[None, :]).astype(jnp.int32), axis=1) - 1
    chosen = seq_of_row[:, None] == seq_ids[None, :]
    positions = row_ids - jnp.sum(jnp.where(chosen, in_start[None, :], 0), axis=1)
    cosine, sine = rotary_tables(positions)
    cos_k, sin_k = cosine[:, None, :], sine[:, None, :]
    cos_q, sin_q = cosine[HALO:, None, None, :], sine[HALO:, None, None, :]

    gain_one = links.both(attn_gain[None, :]).astype(F32)
    gain_two = ffn_gain.astype(F32)[None, :]
    rms_one = lax.rsqrt(jnp.mean(tokens_ext * tokens_ext, axis=-1, keepdims=True) + EPSILON)
    normed_attn = (tokens_ext * rms_one * gain_one).astype(BF16)

    q_width, k_width = w_query.shape[1], w_key.shape[1]
    kv_local = k_width // HD
    repeats = q_width // k_width
    ext = HALO + count
    w_q = attn_all[:, :q_width]
    w_kv = attn_all[:, q_width : q_width + 2 * k_width]
    w_out_t = attn_all[:, q_width + 2 * k_width :]
    queries = matmul(normed_attn[HALO:], w_q).reshape(count, kv_local, repeats, HD)
    keys_values = matmul(normed_attn, w_kv)
    keys = keys_values[:, :k_width].reshape(ext, kv_local, HD)
    values = keys_values[:, k_width:].astype(BF16).reshape(ext, kv_local, HD)
    queries_rot = rotate(queries, cos_q, sin_q).astype(BF16)
    keys_rot = rotate(keys, cos_k, sin_k).astype(BF16)
    allowed = (seq_of_row[HALO:, None] == seq_of_row[None, :]) & (
        row_ids[HALO:, None] >= row_ids[None, :]
    )
    scores = jnp.einsum("qgrd,kgd->grqk", queries_rot, keys_rot, preferred_element_type=F32)
    scores = jnp.where(allowed[None, None], scores * HD ** (-0.5), -1e30)
    highest = jnp.max(scores, axis=-1, keepdims=True)
    expo = jnp.exp(scores - highest)
    probs = expo / jnp.sum(expo, axis=-1, keepdims=True)
    probs_low = probs.astype(BF16)
    attended = jnp.einsum("grqk,kgd->qgrd", probs_low, values, preferred_element_type=F32)
    attended = attended.astype(BF16).reshape(count, q_width)
    out_mine, out_theirs = links.halves(matmul_t(attended, w_out_t))
    tokens_half = tokens.astype(F32)
    mixed = tokens_half + (out_mine + links.swap(out_theirs))

    def row_sum(x):
        total = jnp.sum(x, axis=-1)[None, :]
        return (total + links.swap(total)).reshape(count, 1)

    rms_two = lax.rsqrt(row_sum(mixed * mixed) / width + EPSILON)
    normed_ffn = links.both(line_gather((mixed * rms_two * gain_two).astype(BF16)))

    gate_up = matmul(normed_ffn, w_gate_up)
    gate, upward = gate_up[:, :chunk], gate_up[:, chunk:]
    sigmoid = jax.nn.sigmoid(gate)
    silu_gate = gate * sigmoid
    hidden = (silu_gate * upward).astype(BF16)
    hidden_grad = matmul(cot_line, w_down_t)
    gate_act_grad = (hidden_grad * upward * sigmoid * (1.0 + gate * (1.0 - sigmoid))).astype(BF16)
    up_act_grad = (hidden_grad * silu_gate).astype(BF16)
    act_grad = jnp.concatenate([gate_act_grad, up_act_grad], axis=1)
    norm_part, act_grad, hidden = lax.optimization_barrier(
        (matmul_t(act_grad, w_gate_up), act_grad, hidden)
    )
    norm_mine, norm_theirs = links.halves(norm_part)
    normed_ffn_grad = line_sum(norm_mine + links.swap(norm_theirs.astype(BF16)).astype(F32))
    ffn_mine_out, ffn_theirs_out = links.halves(matmul_t(hidden, w_down_t))
    ffn_out = line_sum(ffn_mine_out + links.swap(ffn_theirs_out.astype(BF16)).astype(F32))
    output = (mixed + ffn_out).astype(BF16)

    down_sum = fold_plane(links, t_matmul(cot_line, hidden).astype(BF16), rows)
    gate_up_sum = fold_plane(links, t_matmul(normed_ffn, act_grad).astype(BF16), rows)
    ffn_sum = jnp.concatenate([gate_up_sum, down_sum], axis=2).astype(BF16)
    ffn_gain_local = jnp.sum(normed_ffn_grad * mixed * rms_two, axis=0)
    inner_two = row_sum(normed_ffn_grad * gain_two * mixed)
    mixed_grad = (
        cotangent.astype(F32)
        + rms_two * gain_two * normed_ffn_grad
        - mixed * rms_two * rms_two * rms_two * inner_two / width
    )

    attn_out_grad = links.both(mixed_grad.astype(BF16))
    out_local = t_matmul(attn_out_grad, attended)
    attended_grad = matmul(attn_out_grad, w_out_t).astype(BF16)
    attended_grad = attended_grad.reshape(count, kv_local, repeats, HD)
    values_grad = jnp.einsum("grqk,qgrd->kgd", probs_low, attended_grad, preferred_element_type=F32)
    values_grad = values_grad.astype(BF16).reshape(ext, k_width)
    probs_grad = jnp.einsum("qgrd,kgd->grqk", attended_grad, values, preferred_element_type=F32)
    scores_grad = (
        probs * (probs_grad - jnp.sum(probs * probs_grad, axis=-1, keepdims=True))
    ).astype(BF16)
    rot_q_grad = jnp.einsum(
        "grqk,kgd->qgrd", scores_grad, keys_rot, preferred_element_type=F32
    ) * HD ** (-0.5)
    rot_k_grad = jnp.einsum(
        "grqk,qgrd->kgd", scores_grad, queries_rot, preferred_element_type=F32
    ) * HD ** (-0.5)
    queries_grad = rotate_back(rot_q_grad, cos_q, sin_q).astype(BF16).reshape(count, q_width)
    keys_grad = rotate_back(rot_k_grad, cos_k, sin_k).astype(BF16).reshape(ext, k_width)
    kv_grad = jnp.concatenate([keys_grad, values_grad], axis=1)
    normed_grad = matmul_t(kv_grad, w_kv)
    normed_grad = normed_grad + jnp.pad(matmul_t(queries_grad, w_q), ((HALO, 0), (0, 0)))
    grad_mine, grad_theirs = links.halves(normed_grad)
    attn_total, ffn_bf16, tokens_grad, gains = finish(
        links.plane,
        t_matmul(normed_attn[HALO:], queries_grad).astype(BF16),
        t_matmul(normed_attn, kv_grad).astype(BF16),
        out_local.astype(BF16),
        ffn_sum,
        grad_mine,
        grad_theirs.astype(BF16),
        mixed_grad,
        tokens,
        rms_one[HALO:],
        attn_gain.astype(F32)[None, :],
        ffn_gain_local[None, :],
    )
    ffn_grads = ffn_bf16.astype(F32)
    share = half_width // n
    gains = lax.dynamic_slice_in_dim(gains[:2], links.index * share, share, 1)
    return (
        output,
        tokens_grad,
        gains[:1],
        attn_total[:, :q_width],
        attn_total[:, q_width : q_width + k_width],
        attn_total[:, q_width + k_width : q_width + 2 * k_width],
        attn_total[:, q_width + 2 * k_width :].T,
        gains[1:],
        ffn_grads[0],
        ffn_grads[1],
        ffn_grads[2].T,
    )


def solution(mesh):
    weight = P("dp", "tensor")
    turned = P("tensor", "dp")
    return jax.shard_map(
        on_device,
        mesh=mesh,
        in_specs=(
            weight, weight, P(), P(), P("tensor"), weight, weight, weight, turned,
            P("tensor"), weight, weight, turned,
        ),
        out_specs=(
            weight, weight, turned, weight, weight, weight, turned, turned, weight, weight, turned,
        ),
        check_vma=False,
    )
```

```python
import functools

import jax
import jax.experimental.pallas as pl
import jax.experimental.pallas.tpu as pltpu
import jax.numpy as jnp
from jax import lax
from jax.sharding import PartitionSpec as P

HD = 256
HALO = 192
LINE = 4

EPSILON = 1e-06
ROPE_BASE = 1000042.0
BF16 = jnp.bfloat16
F32 = jnp.float32
MESH = pl.DeviceIdType.MESH
ANY = pl.BlockSpec(memory_space=pl.ANY)


def matmul(left, right):
    return jnp.dot(left, right, preferred_element_type=F32)


def matmul_t(left, right):
    return lax.dot_general(left, right, (((1,), (1,)), ((), ())), preferred_element_type=F32)


def t_matmul(left, right):
    return lax.dot_general(left, right, (((0,), (0,)), ((), ())), preferred_element_type=F32)


def rotary_tables(positions):
    exponents = jnp.arange(0, HD, 2).astype(F32) / HD
    inverse = jnp.power(F32(ROPE_BASE), -exponents)
    angles = positions.astype(F32)[:, None] * inverse[None, :]
    angles = jnp.concatenate([angles, angles], axis=1)
    return (jnp.cos(angles), jnp.sin(angles))


def rotate(vectors, cosine, sine):
    middle = vectors.shape[-1] // 2
    turned = jnp.concatenate([-vectors[..., middle:], vectors[..., :middle]], axis=-1)
    return vectors * cosine + turned * sine


def rotate_back(grads, cosine, sine):
    middle = grads.shape[-1] // 2
    scaled = grads * sine
    turned = jnp.concatenate([scaled[..., middle:], -scaled[..., :middle]], axis=-1)
    return grads * cosine + turned


class Links:
    def __init__(self):
        self.count = lax.axis_size("dp")
        self.plane = self.count // LINE
        self.index = lax.axis_index("dp")
        self.line, self.place = self.index // self.plane, self.index % self.plane
        self.half = lax.axis_index("tensor")
        self.bits = [1 << b for b in range(self.plane.bit_length() - 1)]

    def step(self, x, k):
        n, shift = self.count, k * self.plane
        return lax.ppermute(x, "dp", [(d, (d + shift) % n) for d in range(n)])

    def cross(self, x, bit):
        return lax.ppermute(x, "dp", [(d, d ^ bit) for d in range(self.count)])

    def swap(self, x):
        return lax.ppermute(x, "tensor", [(0, 1), (1, 0)])

    def both(self, x):
        other = self.swap(x)
        first = self.half == 0
        return jnp.concatenate([jnp.where(first, x, other), jnp.where(first, other, x)], axis=1)

    def halves(self, x):
        width = x.shape[1] // 2
        mine = lax.dynamic_slice_in_dim(x, self.half * width, width, 1)
        theirs = lax.dynamic_slice_in_dim(x, (1 - self.half) * width, width, 1)
        return mine, theirs

    def order(self, turn):
        return self.bits[turn % len(self.bits):] + self.bits[: turn % len(self.bits)]

    def spread(self, x, turn):
        held = {0: x}
        for bit in self.order(turn):
            held |= {key | bit: self.cross(part, bit) for key, part in held.items()}
        return held

    def fold(self, held, turn):
        for bit in self.order(turn):
            kept = {key: part for key, part in held.items() if not key & bit}
            for key in kept:
                got = self.cross(held[key | bit].astype(BF16), bit)
                kept[key] = kept[key].astype(F32) + got.astype(F32)
            held = kept
        return held[0]


def flip(place, key):
    bit = 1
    while bit <= key:
        if key & bit:
            place = place + bit * (1 - 2 * lax.rem(lax.div(place, bit), 2))
        bit *= 2
    return place


def forward_kernel(plane, wq, wk, wv, wo, wg, wu, wd, tok, cot, gain, gain_two, cos, sin, bias,
                   attn_out, ffn, normed_line, cot_line, normed, rms, q_rot, k_rot, values, attended, mixed, rms_two,
                   attn, ext, gains, out_send, out_recv, square, square_in, normed_two,
                   own_sem, zs, zr, ps, pr, fs, fr, qs, qr, ts, tr, ns, nr, cs, cr, es, er):
    rows, tok_rows, width = wq.shape[0], tok.shape[0], tok.shape[1]
    count = plane * LINE
    halo = ext.shape[0] - tok_rows
    chunk = wd.shape[1] // LINE
    bits = [1 << b for b in range(plane.bit_length() - 1)]
    device, half = lax.axis_index("dp"), lax.axis_index("tensor")
    line, place = lax.div(device, plane), lax.rem(device, plane)

    greet = [lax.rem(line + k, LINE) * plane + place for k in range(1, LINE)]
    greet += [line * plane + flip(place, bit) for bit in bits]
    greet += [lax.rem(device + 1, count), lax.rem(device + count - 1, count)]
    barrier = pltpu.get_barrier_semaphore()
    for peer in greet:
        pl.semaphore_signal(barrier, 1, device_id=(peer, half), device_id_type=MESH)
    pl.semaphore_signal(barrier, 1, device_id=(device, 1 - half), device_id_type=MESH)

    def remote(src, dst, sent, got, peer, core=half):
        return pltpu.make_async_remote_copy(
            src_ref=src, dst_ref=dst, send_sem=sent, recv_sem=got,
            device_id=(peer, core), device_id_type=MESH,
        )

    def across(src, dst, j):
        return remote(src, dst, es.at[j], er.at[j], device, 1 - half)

    mine = pl.ds(pl.multiple_of(device * rows, rows), rows)
    own, at = [], 0

    def keep(src, dst):
        own.append(pltpu.make_async_copy(src, dst, own_sem.at[len(own)]))

    for block in (wq, wk, wv, wo):
        wide = block.shape[1]
        keep(block, attn.at[mine, pl.ds(at, wide)])
        at += wide

    def hidden(block, member):
        return block.at[:, pl.ds(pl.multiple_of(member * chunk, chunk), chunk)]

    for j, block in enumerate((wg, wu, wd)):
        keep(hidden(block, line), ffn.at[mine, pl.ds(j * chunk, chunk)])
    features = pl.ds(pl.multiple_of(half * width, width), width)
    others = pl.ds(pl.multiple_of((1 - half) * width, width), width)
    keep(tok, ext.at[pl.ds(halo, tok_rows), features])

    def line_rows(member):
        return pl.ds(pl.multiple_of(member * tok_rows, tok_rows), tok_rows)

    keep(cot, cot_line.at[line_rows(line), features])
    keep(gain, gains.at[:, features])
    for copy in own:
        copy.start()
    first = pltpu.make_async_copy(
        tok.at[pl.ds(0, halo)], ext.at[pl.ds(0, halo), features], own_sem.at[len(own)]
    )
    pl.semaphore_wait(barrier, len(greet) + 1)

    tok_cross = across(tok, ext.at[pl.ds(halo, tok_rows), features], 0)
    gain_cross = across(gain, gains.at[:, features], 1)
    tok_next = remote(
        tok.at[pl.ds(tok_rows - halo, halo)], ext.at[pl.ds(0, halo), features], ts.at[0], tr.at[0], device + 1
    )
    tok_relay = across(ext.at[pl.ds(0, halo), features], ext.at[pl.ds(0, halo), features], 2)
    cot_cross = across(cot, cot_line.at[line_rows(line), features], 3)
    for copy in own[:4]:
        copy.wait()

    def line_copy(origin, step):
        block = attn.at[pl.ds(pl.multiple_of((origin * plane + place) * rows, rows), rows)]
        return remote(block, block, zs.at[(step + 1) // 2, origin], zr.at[origin], device + step * plane)

    part = rows // 2

    def keys_after(turn, stage):
        keys = [0]
        for bit in (bits[turn:] + bits[:turn])[:stage]:
            keys += [key | bit for key in keys]
        return keys

    def plane_copy(whole, sent, got, origin, turn, key, bit):
        block = whole.at[
            pl.ds(pl.multiple_of((origin * plane + flip(place, key)) * rows + turn * part, part), part)
        ]
        sems = [s.at[origin, turn, key | bit] for s in (sent, got)]
        return remote(block, block, *sems, line * plane + flip(place, bit))

    def spread(which, origin, stage):
        for turn in range(2):
            order = bits[turn:] + bits[:turn]
            if stage:
                for key in keys_after(turn, stage - 1):
                    plane_copy(*which, origin, turn, key, order[stage - 1]).wait_recv()
            if stage < len(bits):
                for key in keys_after(turn, stage):
                    plane_copy(*which, origin, turn, key, order[stage]).start()

    def spread_sent(which):
        for origin in range(LINE):
            for turn in range(2):
                for stage, bit in enumerate(bits[turn:] + bits[:turn]):
                    for key in keys_after(turn, stage):
                        plane_copy(*which, origin, turn, key, bit).wait_send()

    attn_plane, ffn_plane = (attn, ps, pr), (ffn, qs, qr)

    def member(k):
        return lax.rem(line + k, LINE)

    def ffn_copies(k):
        return [
            remote(
                hidden(block, member(k)), ffn.at[mine, pl.ds(j * chunk, chunk)],
                fs.at[k - 1, j], fr.at[k - 1, j], member(k) * plane + place,
            )
            for j, block in enumerate((wg, wu, wd))
        ]

    def line_send(src, whole, sent, got, k):
        return remote(src, whole.at[line_rows(line), features], sent.at[k - 1], got.at[k - 1], member(k) * plane + place)

    def line_relay(whole, j, k):
        block = whole.at[line_rows(member(LINE - k)), features]
        return across(block, block, j + k - 1)

    slots = [(line, None, None)]
    for d in range(1, LINE):
        slots += [(line - d, line >= d, 1), (line + d, line + d < LINE, -1)]

    def guarded(condition, action):
        if condition is None:
            action()
        else:
            pl.when(condition)(action)

    def arrive(origin, step):
        if step is not None:
            line_copy(origin, step).wait_recv()
        if step in (None, 1):
            pl.when(line < LINE - 1)(lambda: line_copy(origin, 1).start())
        if step in (None, -1):
            pl.when(line > 0)(lambda: line_copy(origin, -1).start())
        spread(attn_plane, origin, 0)

    step = 16

    def block_rows(i, start=0):
        return pl.ds(pl.multiple_of(start + i * step, step), step)

    def norm_one(start):
        def body(i, carry):
            at = block_rows(i, start)
            x = ext[at].astype(F32)
            r = lax.rsqrt(jnp.mean(x * x, axis=1, keepdims=True) + EPSILON)
            normed[at] = (x * r * gains[:1]).astype(BF16)
            if start:
                rms[block_rows(i)] = r
            return carry

        lax.fori_loop(0, (tok_rows if start else halo) // step, body, 0)

    pl.when(device < count - 1)(lambda: tok_next.start())
    for j in range(len(slots) + len(bits)):
        if j < len(slots):
            origin, condition, direction = slots[j]
            guarded(condition, functools.partial(arrive, origin, direction))
        if j == 0:
            tok_cross.start()
            gain_cross.start()
        if j == len(slots) - 1:
            for k in (1, 3, 2):
                for copy in ffn_copies(k):
                    copy.start()
            cot_cross.start()
            for k in range(1, LINE):
                line_send(cot, cot_line, cs, cr, k).start()
        for stage in range(1, len(bits) + 1):
            if 0 <= j - stage < len(slots):
                origin, condition, direction = slots[j - stage]
                if j == len(slots) + len(bits) - 1 and stage == len(bits):
                    for copy in own[4:7]:
                        copy.wait()
                    spread(ffn_plane, line, 0)
                guarded(condition, functools.partial(spread, attn_plane, origin, stage))
        if j == 1:
            pl.when(device == 0)(lambda: first.start())
            pl.when(device == 0)(lambda: first.wait())
            pl.when(device > 0)(lambda: tok_next.wait_recv())
            tok_relay.start()
        if j == 3:
            tok_cross.wait()
            gain_cross.wait()
            tok_relay.wait()
            for copy in own[7:]:
                copy.wait()
            norm_one(0)
            norm_one(halo)

    kept = pltpu.make_async_copy(attn, attn_out, own_sem.at[len(own) + 1])
    kept.start()

    arrivals = (0, 1, 3, 2)

    def ffn_arrive(k):
        for copy in ffn_copies(k):
            copy.wait_recv()
        spread(ffn_plane, member(LINE - k), 0)

    q_width, k_width = wq.shape[1], wk.shape[1]
    kv_local, repeats = k_width // HD, q_width // k_width

    def turn_by(x, start, size):
        turned = jnp.concatenate([-x[:, HD // 2 :], x[:, : HD // 2]], axis=1)
        return (x * cos[pl.ds(start, size)] + turned * sin[pl.ds(start, size)]).astype(BF16)

    whole_rows = normed.shape[0]
    for j in range(kv_local):
        at = pl.ds(j * HD, HD)
        key_block = matmul(normed[...], attn[:, pl.ds(q_width + j * HD, HD)])
        k_rot[:, at] = turn_by(key_block, 0, whole_rows)
        values[:, at] = matmul(normed[...], attn[:, pl.ds(q_width + k_width + j * HD, HD)]).astype(BF16)
        if j == 0:
            ffn_arrive(1)
            ffn_arrive(3)
        for r in range(repeats):
            head = pl.ds((j * repeats + r) * HD, HD)
            query = matmul(normed[pl.ds(halo, tok_rows)], attn[:, head])
            q_rot[:, head] = turn_by(query, halo, tok_rows)
            scores = matmul_t(q_rot[:, head], k_rot[:, at]) * HD ** (-0.5) + bias[...]
            expo = jnp.exp(scores - jnp.max(scores, axis=1, keepdims=True))
            probs = expo / jnp.sum(expo, axis=1, keepdims=True)
            attended[:, head] = matmul(probs.astype(BF16), values[:, at]).astype(BF16)
        if j == 0:
            ffn_arrive(2)
            for stage in range(1, len(bits)):
                spread(ffn_plane, line, stage)

    out_at = pl.ds(q_width + 2 * k_width, q_width)
    tiles = width // 256
    for tile in range(tiles):
        block = attn[pl.ds(pl.multiple_of((1 - half) * width + tile * 256, 256), 256), out_at]
        out_send[:, pl.ds(tile * 256, 256)] = matmul_t(attended[...], block)
    out_cross = across(out_send, out_recv, 4)
    out_cross.start()
    for tile in range(tiles):
        block = attn[pl.ds(pl.multiple_of(half * width + tile * 256, 256), 256), out_at]
        mixed[:, pl.ds(tile * 256, 256)] = matmul_t(attended[...], block)
    for stage in range(1, len(bits)):
        spread(ffn_plane, member(LINE - 1), stage)
    out_cross.wait()

    def mix(i, carry):
        at = block_rows(i)
        value = ext[block_rows(i, halo), features].astype(F32) + (mixed[at] + out_recv[at])
        mixed[at] = value
        square[at] = jnp.broadcast_to(jnp.sum(value * value, axis=1, keepdims=True), (step, square.shape[1]))
        return carry

    lax.fori_loop(0, tok_rows // step, mix, 0)
    square_cross = across(square, square_in, 5)
    square_cross.start()
    square_cross.wait()

    def norm_two(i, carry):
        at = block_rows(i)
        r = lax.rsqrt((square[at] + square_in[at])[:, :1] / (2 * width) + EPSILON)
        rms_two[at] = r
        normed_two[at] = (mixed[at] * r * gain_two[...]).astype(BF16)
        return carry

    lax.fori_loop(0, tok_rows // step, norm_two, 0)
    normed_own = pltpu.make_async_copy(
        normed_two, normed_line.at[line_rows(line), features], own_sem.at[len(own) + 2]
    )
    normed_own.start()
    for k in range(1, LINE):
        line_send(normed_two, normed_line, ns, nr, k).start()
    normed_cross = across(normed_two, normed_line.at[line_rows(line), features], 6)
    normed_cross.start()

    for k in range(1, LINE):
        line_send(cot, cot_line, cs, cr, k).wait_recv()
        line_relay(cot_line, 7, k).start()
    for k in arrivals[2:]:
        for stage in range(1, len(bits)):
            spread(ffn_plane, member(LINE - k), stage)
    for k in range(1, LINE):
        line_send(normed_two, normed_line, ns, nr, k).wait_recv()
        line_relay(normed_line, 7 + LINE - 1, k).start()
    for k in arrivals:
        spread(ffn_plane, member(LINE - k), len(bits))

    for origin in range(LINE):
        pl.when((origin <= line) & (line < LINE - 1))(lambda o=origin: line_copy(o, 1).wait_send())
        pl.when((origin >= line) & (line > 0))(lambda o=origin: line_copy(o, -1).wait_send())
    spread_sent(attn_plane)
    spread_sent(ffn_plane)
    for k in range(1, LINE):
        for copy in ffn_copies(k):
            copy.wait_send()
        line_send(cot, cot_line, cs, cr, k).wait_send()
        line_send(normed_two, normed_line, ns, nr, k).wait_send()
        line_relay(cot_line, 7, k).wait()
        line_relay(normed_line, 7 + LINE - 1, k).wait()
    pl.when(device < count - 1)(lambda: tok_next.wait_send())
    cot_cross.wait()
    normed_cross.wait()
    normed_own.wait()
    kept.wait()


def forward(plane, wq, wk, wv, wo, wg, wu, wd, tokens, cotangent, gain, gain_two, cos, sin, bias):
    rows, (count, half_width) = wq.shape[0], tokens.shape
    chunk = wd.shape[1] // LINE
    columns = sum(w.shape[1] for w in (wq, wk, wv, wo))
    width, whole, ext = 2 * half_width, LINE * plane * rows, HALO + count
    dma, vmem, shape = pltpu.SemaphoreType.DMA, pltpu.VMEM, jax.ShapeDtypeStruct
    inside = pl.BlockSpec(memory_space=pltpu.VMEM)
    pairs = [(LINE, 2, plane)] * 2 + [(LINE - 1, 3)] * 2 + [(LINE, 2, plane)] * 2
    pairs += [(1,)] * 2 + [(LINE - 1,)] * 4 + [(7 + 2 * (LINE - 1),)] * 2
    return pl.pallas_call(
        functools.partial(forward_kernel, plane),
        out_shape=(
            shape((whole, columns), BF16), shape((whole, 3 * chunk), BF16),
            shape((LINE * count, width), BF16), shape((LINE * count, width), BF16),
            shape((ext, width), BF16), shape((count, 1), F32), shape((count, wq.shape[1]), BF16),
            shape((ext, wk.shape[1]), BF16), shape((ext, wk.shape[1]), BF16), shape((count, wq.shape[1]), BF16),
            shape((count, half_width), F32), shape((count, 1), F32),
        ),
        in_specs=[ANY] * 9 + [inside] * 5,
        out_specs=[ANY] * 4 + [inside] * 8,
        scratch_shapes=[
            vmem((whole, columns), BF16), vmem((ext, width), BF16), vmem((8, width), F32),
            vmem((count, half_width), F32), vmem((count, half_width), F32), vmem((count, 128), F32),
            vmem((count, 128), F32), vmem((count, half_width), BF16),
            dma((14,)), dma((2, LINE)), dma((LINE,)), *[dma(p) for p in pairs],
        ],
        compiler_params=pltpu.CompilerParams(
            collective_id=1, has_side_effects=True, vmem_limit_bytes=60 * 2**20
        ),
    )(wq, wk, wv, wo, wg, wu, wd, tokens, cotangent, gain, gain_two, cos, sin, bias)


def fold_plan(bits, turn):
    order, plan, slot = bits[turn:] + bits[:turn], [], 0
    for stage, bit in enumerate(order):
        keys = [0]
        for later in order[stage + 1 :]:
            keys += [key | later for key in keys]
        plan.append((bit, keys, slot))
        slot += len(keys)
    return plan


def finish_kernel(plane, gq, gkv, go, fsum, grad_mine, grad_theirs, mixed_grad, tok, rms, gain, gain_two,
                  total, fout, tok_grad, gains,
                  recv, sendbuf, acc, zsend, zrecv, gx, hsend, hrecv, nag, inner, inner_in, gbuf, gin,
                  own_sem, s0, r0, zs, zr, fs, fr, cs, cr, gs, gr):
    rows = total.shape[0]
    segment = gq.shape[1]
    count = plane * LINE
    tok_rows, width = tok.shape
    halo = grad_mine.shape[0] - tok_rows
    chunk = fsum.shape[2] // 3
    part = rows // 2
    bits = [1 << b for b in range(plane.bit_length() - 1)]
    device, half = lax.axis_index("dp"), lax.axis_index("tensor")
    line, place = lax.div(device, plane), lax.rem(device, plane)

    greet = [lax.rem(line + k, LINE) * plane + place for k in range(1, LINE)]
    greet += [line * plane + flip(place, bit) for bit in bits]
    greet += [lax.rem(device + 1, count), lax.rem(device + count - 1, count)]
    barrier = pltpu.get_barrier_semaphore()
    for peer in greet:
        pl.semaphore_signal(barrier, 1, device_id=(peer, half), device_id_type=MESH)
    pl.semaphore_signal(barrier, 1, device_id=(device, 1 - half), device_id_type=MESH)

    def remote(src, dst, sent, got, peer, core=half):
        return pltpu.make_async_remote_copy(
            src_ref=src, dst_ref=dst, send_sem=sent, recv_sem=got,
            device_id=(peer, core), device_id_type=MESH,
        )

    def member(c):
        return lax.rem(line + c, LINE)

    def hidden(origin):
        return pl.ds(pl.multiple_of(origin * chunk, chunk), chunk)

    def ffn_copy(c, j):
        return remote(
            fsum.at[member(c), :, pl.ds(j * chunk, chunk)], fout.at[j, :, hidden(line)],
            fs.at[c - 1, j], fr.at[c - 1, j], member(c) * plane + place,
        )

    own = [
        pltpu.make_async_copy(fsum.at[line, :, pl.ds(j * chunk, chunk)], fout.at[j, :, hidden(line)], own_sem.at[j])
        for j in range(3)
    ]
    for copy in own:
        copy.start()
    pl.semaphore_wait(barrier, len(greet) + 1)

    plans = [fold_plan(bits, turn) for turn in range(2)]
    stages, later = len(bits), plane // 2

    def raw(ref, c, turn, key):
        at = (member(c) * plane + flip(place, key)) * rows + turn * part
        return ref.at[pl.ds(pl.multiple_of(at, part), part)]

    def fold_copies(c, turn, stage):
        bit, keys, slot = plans[turn][stage]
        peer = line * plane + flip(place, bit)
        out = []
        for j, key in enumerate(keys):
            sems = (s0.at[c, turn, slot + j], r0.at[c, turn, slot + j])
            dst = recv.at[c, turn, slot + j]
            if stage == 0:
                for g, ref in enumerate((gq, gkv, go)):
                    out.append(remote(raw(ref, c, turn, key | bit), dst.at[:, pl.ds(g * segment, segment)], *sems, peer))
            else:
                out.append(remote(sendbuf.at[c, turn, slot - later + j], dst, *sems, peer))
        return out

    def fold_wait(c, turn, stage, sent):
        bit, keys, slot = plans[turn][stage]
        for j in range(len(keys)):
            whole = recv.at[c, turn, slot + j]
            copy = remote(whole, whole, s0.at[c, turn, slot + j], r0.at[c, turn, slot + j], line * plane + flip(place, bit))
            if sent:
                copy.wait_send()
            else:
                copy.wait_recv()

    step = 16

    def fold_add(c, turn, stage):
        bit, keys, slot = plans[turn][stage]
        last = stage == len(plans[turn]) - 1
        sends = {}
        if not last:
            next_bit, next_keys, next_slot = plans[turn][stage + 1]
            sends = {key | next_bit: next_slot - later + j for j, key in enumerate(next_keys)}

        def body(i, carry):
            at = pl.ds(pl.multiple_of(i * step, step), step)
            for j, key in enumerate(keys):
                for g, ref in enumerate((gq, gkv, go)):
                    columns = pl.ds(g * segment, segment)
                    got = recv[c, turn, slot + j, at, columns].astype(F32)
                    if stage == 0:
                        had = raw(ref, c, turn, key)[at, :].astype(F32)
                    else:
                        had = acc[c, turn, key_slot[key], at, columns]
                    value = had + got
                    if last and c:
                        zsend[c - 1, pl.ds(pl.multiple_of(turn * part + i * step, step), step), columns] = value.astype(BF16)
                    elif last:
                        total[pl.ds(pl.multiple_of(turn * part + i * step, step), step), columns] = value
                    elif key in sends:
                        sendbuf[c, turn, sends[key], at, columns] = value.astype(BF16)
                    else:
                        acc[c, turn, key_slot[key], at, columns] = value
            return carry

        stay = [key for key in plans[turn][0][1] if not key & plans[turn][min(1, stages - 1)][0]]
        key_slot = {key: j for j, key in enumerate(stay)}
        lax.fori_loop(0, part // step, body, 0)

    def z_copy(c, turn):
        at = pl.ds(turn * part, part)
        return remote(
            zsend.at[c - 1, at], zrecv.at[c - 1, at], zs.at[c - 1, turn], zr.at[c - 1, turn], member(c) * plane + place
        )

    core_copy = remote(grad_theirs, gx, cs.at[0], cr.at[0], device, 1 - half)
    halo_copy = remote(hsend, hrecv, cs.at[1], cr.at[1], device - 1)
    inner_copy = remote(inner, inner_in, cs.at[2], cr.at[2], device, 1 - half)
    core_copy.start()

    turns = (2, 1, 3, 0)

    def start(c, stage):
        for turn in range(2):
            for copy in fold_copies(c, turn, stage):
                copy.start()

    start(turns[0], 0)
    start(turns[1], 0)
    for c in range(1, LINE):
        for j in range(3):
            ffn_copy(c, j).start()

    core_copy.wait()

    def rows_of(i):
        return pl.ds(pl.multiple_of(i * step, step), step)

    def add_halo(i, carry):
        hsend[rows_of(i)] = (grad_mine[rows_of(i)] + gx[rows_of(i)].astype(F32)).astype(BF16)
        return carry

    def add_own(i, carry):
        at = pl.ds(pl.multiple_of(halo + i * step, step), step)
        nag[rows_of(i)] = grad_mine[at] + gx[at].astype(F32)
        return carry

    def add_behind(i, carry):
        at = pl.ds(pl.multiple_of(tok_rows - halo + i * step, step), step)
        nag[at] = nag[at] + hrecv[rows_of(i)].astype(F32)
        return carry

    def local_sums(i, carry):
        at = rows_of(i)
        grad, x = nag[at], tok[at].astype(F32)
        weighted = jnp.sum(grad * gain[...] * x, axis=1, keepdims=True)
        inner[at] = jnp.broadcast_to(weighted, (step, inner.shape[1]))
        product = grad * x * rms[at]
        return carry + product[:8] + product[8:]

    def last_norm(i, carry):
        at = rows_of(i)
        r = rms[at]
        whole = (inner[at] + inner_in[at])[:, :1]
        value = mixed_grad[at] + r * gain[...] * nag[at] - tok[at].astype(F32) * (r * r * r * whole / (2 * width))
        tok_grad[at] = value.astype(BF16)
        return carry

    def norm_first():
        lax.fori_loop(0, halo // step, add_halo, 0)
        pl.when(device > 0)(lambda: halo_copy.start())
        lax.fori_loop(0, tok_rows // step, add_own, 0)

    def norm_second():
        @pl.when(device < count - 1)
        def _():
            halo_copy.wait_recv()
            lax.fori_loop(0, halo // step, add_behind, 0)

        sums = lax.fori_loop(0, tok_rows // step, local_sums, jnp.zeros((8, width), F32))
        gbuf[...] = jnp.concatenate(
            [jnp.sum(sums, axis=0, keepdims=True), gain_two[...], jnp.zeros((6, width), F32)], axis=0
        )
        inner_copy.start()

    def gain_copy(j):
        peer = line * plane + flip(place, bits[j]) if j < stages else member(j - stages + 1) * plane + place
        return remote(gbuf, gin.at[j], gs.at[j], gr.at[j], peer)

    def norm_third():
        inner_copy.wait()
        lax.fori_loop(0, tok_rows // step, last_norm, 0)

    norm_first()

    pending = []
    for j in range(len(turns) + stages):
        if j < len(turns):
            if j + 2 < len(turns):
                start(turns[j + 2], 0)
        for stage in range(stages):
            if 0 <= j - stage < len(turns):
                c = turns[j - stage]
                for turn in range(2):
                    fold_wait(c, turn, stage, False)
                    fold_add(c, turn, stage)
                    if stage + 1 < stages:
                        for copy in fold_copies(c, turn, stage + 1):
                            copy.start()
                    elif c:
                        z_copy(c, turn).start()
        if j == 0:
            norm_second()
        elif j <= stages:
            if j > 1:
                gain_copy(j - 2).wait()
                gbuf[...] = gbuf[...] + gin[j - 2]
            gain_copy(j - 1).start()
            if j == 1:
                norm_third()

    gain_copy(stages - 1).wait()
    gbuf[...] = gbuf[...] + gin[stages - 1]
    for k in range(stages, stages + LINE - 1):
        gain_copy(k).start()
    for k in range(stages, stages + LINE - 1):
        gain_copy(k).wait()
    gains[...] = gbuf[...] + sum(gin[k] for k in range(stages, stages + LINE - 1))

    for c in range(1, LINE):
        for turn in range(2):
            z_copy(c, turn).wait()

    def add_line(i, carry):
        at = rows_of(i)
        total[at] = total[at] + sum(zrecv[c, at].astype(F32) for c in range(LINE - 1))
        return carry

    lax.fori_loop(0, rows // step, add_line, 0)
    for c in range(LINE):
        for turn in range(2):
            for stage in range(stages):
                fold_wait(c, turn, stage, True)
    for c in range(1, LINE):
        for j in range(3):
            ffn_copy(c, j).wait()
    pl.when(device > 0)(lambda: halo_copy.wait_send())
    for copy in own:
        copy.wait()


def finish(plane, gq, gkv, go, fsum, grad_mine, grad_theirs, mixed_grad, tok, rms, gain, gain_two):
    columns = 3 * gq.shape[1]
    rows, chunk = fsum.shape[1], fsum.shape[2] // 3
    part = rows // 2
    tok_rows, width = tok.shape
    bits = plane.bit_length() - 1
    dma, vmem = pltpu.SemaphoreType.DMA, pltpu.VMEM
    kept = plane - 1
    inside = pl.BlockSpec(memory_space=pltpu.VMEM)
    return pl.pallas_call(
        functools.partial(finish_kernel, plane),
        out_shape=(
            jax.ShapeDtypeStruct((rows, columns), F32),
            jax.ShapeDtypeStruct((3, rows, LINE * chunk), BF16),
            jax.ShapeDtypeStruct((tok_rows, width), BF16),
            jax.ShapeDtypeStruct((8, width), F32),
        ),
        in_specs=[inside] * 3 + [ANY] + [inside] * 7,
        out_specs=[inside, ANY, inside, inside],
        scratch_shapes=[
            vmem((LINE, 2, kept, part, columns), BF16), vmem((LINE, 2, kept - plane // 2, part, columns), BF16),
            vmem((LINE, 2, plane // 4, part, columns), F32), vmem((LINE - 1, rows, columns), BF16),
            vmem((LINE - 1, rows, columns), BF16), vmem(grad_theirs.shape, BF16), vmem((HALO, width), BF16),
            vmem((HALO, width), BF16), vmem((tok_rows, width), F32), vmem((tok_rows, 128), F32),
            vmem((tok_rows, 128), F32), vmem((8, width), F32), vmem((bits + LINE - 1, 8, width), F32),
            dma((3,)), dma((LINE, 2, kept)), dma((LINE, 2, kept)), dma((LINE - 1, 2)), dma((LINE - 1, 2)),
            dma((LINE - 1, 3)), dma((LINE - 1, 3)), dma((3,)), dma((3,)),
            dma((bits + LINE - 1,)), dma((bits + LINE - 1,)),
        ],
        compiler_params=pltpu.CompilerParams(
            collective_id=2, has_side_effects=True, vmem_limit_bytes=60 * 2**20
        ),
    )(gq, gkv, go, fsum, grad_mine, grad_theirs, mixed_grad, tok, rms, gain, gain_two)


def fold_plane(links, grads, rows):
    columns = grads.shape[1]
    parts = grads.reshape(LINE, links.plane, rows, columns)
    out = []
    for turn in range(2):
        half = parts[turn * 2 : turn * 2 + 2]
        held = {
            key: lax.dynamic_slice_in_dim(half, flip(links.place, key), 1, 1)[:, 0]
            for key in range(links.plane)
        }
        out.append(links.fold(held, turn))
    return jnp.concatenate(out, axis=0)


def on_device(
    tokens,
    cotangent,
    lengths,
    order,
    attn_gain,
    w_query,
    w_key,
    w_value,
    w_output,
    ffn_gain,
    w_gate,
    w_up,
    w_down,
):
    links = Links()
    half_index = links.half
    count, half_width = tokens.shape
    width = 2 * half_width
    rows = w_query.shape[0]
    ff_half = w_gate.shape[1]
    chunk = ff_half // LINE

    n = links.count
    ext = HALO + count
    q_width, k_width = w_query.shape[1], w_key.shape[1]
    kv_local, repeats = k_width // HD, q_width // k_width
    seq_ids = jnp.arange(lengths.shape[0])
    in_start = jnp.sum(jnp.where(seq_ids[None, :] < seq_ids[:, None], lengths[None, :], 0), axis=1)
    row_ids = links.index * count - HALO + jnp.arange(ext)
    seq_of_row = jnp.sum((row_ids[:, None] >= in_start[None, :]).astype(jnp.int32), axis=1) - 1
    chosen = seq_of_row[:, None] == seq_ids[None, :]
    positions = row_ids - jnp.sum(jnp.where(chosen, in_start[None, :], 0), axis=1)
    cosine, sine = rotary_tables(positions)
    allowed = (seq_of_row[HALO:, None] == seq_of_row[None, :]) & (
        row_ids[HALO:, None] >= row_ids[None, :]
    )
    bias = jnp.where(allowed, 0.0, -1e30).astype(F32)
    gain_mine = attn_gain.astype(F32)[None, :]
    gain_two = ffn_gain.astype(F32)[None, :]
    (
        attn_all, ffn_all, normed_ffn, cot_line, normed_attn, rms_mine, queries_rot, keys_rot, values,
        attended, mixed, rms_two,
    ) = forward(
        links.plane, w_query, w_key, w_value, w_output.T, w_gate, w_up, w_down.T, tokens, cotangent,
        jnp.broadcast_to(gain_mine, (8, half_width)), gain_two, cosine, sine, bias,
    )
    w_gate_up, w_down_t = ffn_all[:, : 2 * chunk], ffn_all[:, 2 * chunk :]
    w_q = attn_all[:, :q_width]
    w_kv = attn_all[:, q_width : q_width + 2 * k_width]
    w_out_t = attn_all[:, q_width + 2 * k_width :]
    cos_k, sin_k = cosine[:, None, :], sine[:, None, :]
    cos_q, sin_q = cosine[HALO:, None, None, :], sine[HALO:, None, None, :]
    queries_rot = queries_rot.reshape(count, kv_local, repeats, HD)
    keys_rot = keys_rot.reshape(ext, kv_local, HD)
    values = values.reshape(ext, kv_local, HD)

    def line_sum(x):
        def of(k):
            return lax.dynamic_slice_in_dim(x, (links.line + k) % LINE * count, count, 0)

        total = of(0).astype(F32)
        for k in range(1, LINE):
            total += links.step(of(k).astype(BF16), k).astype(F32)
        return total

    def row_sum(x):
        total = jnp.sum(x, axis=-1)[None, :]
        return (total + links.swap(total)).reshape(count, 1)

    gate_up = matmul(normed_ffn, w_gate_up)
    gate, upward = gate_up[:, :chunk], gate_up[:, chunk:]
    sigmoid = jax.nn.sigmoid(gate)
    silu_gate = gate * sigmoid
    hidden = (silu_gate * upward).astype(BF16)
    hidden_grad = matmul(cot_line, w_down_t)
    gate_act_grad = (hidden_grad * upward * sigmoid * (1.0 + gate * (1.0 - sigmoid))).astype(BF16)
    up_act_grad = (hidden_grad * silu_gate).astype(BF16)
    act_grad = jnp.concatenate([gate_act_grad, up_act_grad], axis=1)
    norm_part, act_grad, hidden = lax.optimization_barrier(
        (matmul_t(act_grad, w_gate_up), act_grad, hidden)
    )
    norm_mine, norm_theirs = links.halves(norm_part)
    normed_ffn_grad = line_sum(norm_mine + links.swap(norm_theirs.astype(BF16)).astype(F32))
    ffn_mine_out, ffn_theirs_out = links.halves(matmul_t(hidden, w_down_t))
    ffn_out = line_sum(ffn_mine_out + links.swap(ffn_theirs_out.astype(BF16)).astype(F32))
    output = (mixed + ffn_out).astype(BF16)

    down_sum = fold_plane(links, t_matmul(cot_line, hidden).astype(BF16), rows)
    gate_up_sum = fold_plane(links, t_matmul(normed_ffn, act_grad).astype(BF16), rows)
    ffn_sum = jnp.concatenate([gate_up_sum, down_sum], axis=2).astype(BF16)
    ffn_gain_local = jnp.sum(normed_ffn_grad * mixed * rms_two, axis=0)
    inner_two = row_sum(normed_ffn_grad * gain_two * mixed)
    mixed_grad = (
        cotangent.astype(F32)
        + rms_two * gain_two * normed_ffn_grad
        - mixed * rms_two * rms_two * rms_two * inner_two / width
    )

    attn_out_grad = links.both(mixed_grad.astype(BF16))
    out_local = t_matmul(attn_out_grad, attended)
    scores = jnp.einsum("qgrd,kgd->grqk", queries_rot, keys_rot, preferred_element_type=F32)
    scores = jnp.where(allowed[None, None], scores * HD ** (-0.5), -1e30)
    expo = jnp.exp(scores - jnp.max(scores, axis=-1, keepdims=True))
    probs = expo / jnp.sum(expo, axis=-1, keepdims=True)
    probs_low = probs.astype(BF16)
    attended_grad = matmul(attn_out_grad, w_out_t).astype(BF16)
    attended_grad = attended_grad.reshape(count, kv_local, repeats, HD)
    values_grad = jnp.einsum("grqk,qgrd->kgd", probs_low, attended_grad, preferred_element_type=F32)
    values_grad = values_grad.astype(BF16).reshape(ext, k_width)
    probs_grad = jnp.einsum("qgrd,kgd->grqk", attended_grad, values, preferred_element_type=F32)
    scores_grad = (
        probs * (probs_grad - jnp.sum(probs * probs_grad, axis=-1, keepdims=True))
    ).astype(BF16)
    rot_q_grad = jnp.einsum(
        "grqk,kgd->qgrd", scores_grad, keys_rot, preferred_element_type=F32
    ) * HD ** (-0.5)
    rot_k_grad = jnp.einsum(
        "grqk,qgrd->kgd", scores_grad, queries_rot, preferred_element_type=F32
    ) * HD ** (-0.5)
    queries_grad = rotate_back(rot_q_grad, cos_q, sin_q).astype(BF16).reshape(count, q_width)
    keys_grad = rotate_back(rot_k_grad, cos_k, sin_k).astype(BF16).reshape(ext, k_width)
    kv_grad = jnp.concatenate([keys_grad, values_grad], axis=1)
    normed_grad = matmul_t(kv_grad, w_kv)
    normed_grad = normed_grad + jnp.pad(matmul_t(queries_grad, w_q), ((HALO, 0), (0, 0)))
    grad_mine, grad_theirs = links.halves(normed_grad)
    attn_total, ffn_bf16, tokens_grad, gains = finish(
        links.plane,
        t_matmul(normed_attn[HALO:], queries_grad).astype(BF16),
        t_matmul(normed_attn, kv_grad).astype(BF16),
        out_local.astype(BF16),
        ffn_sum,
        grad_mine,
        grad_theirs.astype(BF16),
        mixed_grad,
        tokens,
        rms_mine,
        gain_mine,
        ffn_gain_local[None, :],
    )
    ffn_grads = ffn_bf16.astype(F32)
    share = half_width // n
    gains = lax.dynamic_slice_in_dim(gains[:2], links.index * share, share, 1)
    return (
        output,
        tokens_grad,
        gains[:1],
        attn_total[:, :q_width],
        attn_total[:, q_width : q_width + k_width],
        attn_total[:, q_width + k_width : q_width + 2 * k_width],
        attn_total[:, q_width + 2 * k_width :].T,
        gains[1:],
        ffn_grads[0],
        ffn_grads[1],
        ffn_grads[2].T,
    )


def solution(mesh):
    weight = P("dp", "tensor")
    turned = P("tensor", "dp")
    return jax.shard_map(
        on_device,
        mesh=mesh,
        in_specs=(
            weight, weight, P(), P(), P("tensor"), weight, weight, weight, turned,
            P("tensor"), weight, weight, turned,
        ),
        out_specs=(
            weight, weight, turned, weight, weight, weight, turned, turned, weight, weight, turned,
        ),
        check_vma=False,
    )
```
